256 devices in a mesh: pair: 32 (over x, y, core), virt: 8 (over z).
Axes of the slice: x: 4, y: 4, z: 8, core: 2. Of those that a mesh axis runs over, the one named last changes fastest.
Arguments:
- amplitudes: bfloat16 [256, 1024, 1024], P(('pair', 'virt')), may hold values from -6 to 6
- lambda_two: bfloat16 [256, 1024, 1024], P(('pair', 'virt')), may hold values from -6 to 6
- lambda_omega: bfloat16 [256, 1024, 1024], P(('pair', 'virt')), may hold values from -6 to 6
- dipole_virtual: bfloat16 [1024, 1024], replicated, may hold values from -0.1875 to 0.1875
- dipole_occupied: float32 [120], replicated, may hold values from -1 to 1
- pair_orbitals: int32 [256, 2], P(('pair', 'virt')), may hold values from 0 to 119
- occupied_spin: int32 [120], replicated, may hold values from 0 to 1
- virtual_spin: int32 [1024], replicated, may hold values from 0 to 1
Outputs:
- response_gram: float32 [256, 256], P(('pair', 'virt'))
The draws below stay inside these ranges and needn't reach their ends.
All inputs are finite; a program needn't handle non-finite values.
Results may differ from the reference program's by a relative error of at most 0.0025.
Values may be sent and summed in bfloat16 or wider, within the bound.
A program may use at most 64 MiB of HBM per device.

```python
import jax
import jax.numpy as jnp
from jax import lax

V = 1024
OCC = 120
PAIRS = 256


def with_ends(entries, rng, least, largest):
    longest = entries.shape.index(max(entries.shape))
    spots = []
    for shift in (0, 1):
        where = [jax.random.randint(jax.random.fold_in(rng, axis), (), 0, length) for axis, length in enumerate(entries.shape)]
        where[longest] = (where[longest] + shift) % entries.shape[longest]
        spots.append(tuple(where))
    return entries.at[spots[0]].set(least).at[spots[1]].set(largest)


def levels(stream_key, dims, shards, low, top_value):
    gain, own = 1.0, jax.random.fold_in(stream_key, 6)
    for dim, shards_of in shards:
        steps = jnp.exp(jax.random.uniform(jax.random.fold_in(own, dim), (shards_of,), jnp.float32, low / len(shards), top_value / len(shards)))
        gain = gain * jnp.repeat(steps, dims[dim] // shards_of).reshape([-1 if axis == dim else 1 for axis in range(len(dims))])
    return gain


def gaussian(key, dims, scale, bound, split=(), kind=jnp.bfloat16):
    values = jax.random.normal(key, dims, jnp.float32) * scale
    if len(split) > 0:
        values = levels(key, dims, split, -0.22, 0.18) * values
    return jnp.clip(values, min=-bound, max=bound).astype(kind)


def setup_inputs(seed: int = 0) -> dict:
    key_list = jax.random.split(jax.random.key(seed), 9)
    return {
        "amplitudes": gaussian(key_list[0], (PAIRS, V, V), 1.0, 6.0, ((0, 256),)),
        "lambda_two": gaussian(key_list[1], (PAIRS, V, V), 1.0, 6.0, ((0, 256),)),
        "lambda_omega": gaussian(key_list[2], (PAIRS, V, V), 1.0, 6.0, ((0, 256),)),
        "dipole_virtual": gaussian(key_list[3], (V, V), V ** -0.5, 0.1875),
        "dipole_occupied": jnp.clip(jax.random.uniform(key_list[4], (OCC,), jnp.float32, -1.0, 1.0), -1.0, 1.0),
        "pair_orbitals": with_ends(jax.random.randint(key_list[5], (PAIRS, 2), 0, OCC), jax.random.fold_in(key_list[5], 1), 0, OCC - 1).astype(jnp.int32),
        "occupied_spin": with_ends(jax.random.randint(key_list[6], (OCC,), 0, 2), jax.random.fold_in(key_list[6], 1), 0, 1).astype(jnp.int32),
        "virtual_spin": with_ends(jax.random.randint(key_list[7], (V,), 0, 2), jax.random.fold_in(key_list[7], 1), 0, 1).astype(jnp.int32),
    }


def commute_pair(args, dipole_virtual, dipole_occupied, occupied_spin, virtual_spin):
    block, orbitals = args
    first_orb = orbitals[0]
    second_orb = orbitals[1]
    first_side = jnp.dot(dipole_virtual, block, preferred_element_type=jnp.float32)
    second_side = jnp.dot(block, dipole_virtual.T, preferred_element_type=jnp.float32)
    shift = dipole_occupied[first_orb] + dipole_occupied[second_orb]
    commutator = first_side + second_side - shift * block.astype(jnp.float32)
    target = occupied_spin[first_orb] + occupied_spin[second_orb]
    allowed = (virtual_spin[:, None] + virtual_spin[None, :]) == target
    commuted = jnp.where(allowed, commutator, jnp.float32(0.0)).astype(jnp.bfloat16)
    masked_amps = jnp.where(allowed, block, jnp.zeros_like(block))
    return commuted, masked_amps


def reference(amplitudes, lambda_two, lambda_omega, dipole_virtual, dipole_occupied, pair_orbitals, occupied_spin, virtual_spin):
    commuted, masked_amps = lax.map(
        lambda args: commute_pair(args, dipole_virtual, dipole_occupied, occupied_spin, virtual_spin),
        (amplitudes, pair_orbitals))
    count = amplitudes.shape[0]
    width = amplitudes.shape[1]
    first_term = jnp.dot(lambda_two.reshape(count, -1), commuted.reshape(count, -1).T, preferred_element_type=jnp.float32)
    second_term = jnp.dot(lambda_omega.reshape(count, -1), masked_amps.reshape(count, -1).T, preferred_element_type=jnp.float32)
    return (first_term + second_term) / jnp.float32(width)
```

```python
import functools

import jax
import jax.numpy as jnp
from jax import lax
from jax.experimental import pallas as pl
from jax.experimental.pallas import tpu as pltpu
from jax.sharding import PartitionSpec as P

MESH = pl.DeviceIdType.MESH
ROWS, LANES = 16, 256
BLOCK = 128
GROUP = 16


def kernel(
    count_pair,
    count_virt,
    amps_hbm,
    two_hbm,
    omega_hbm,
    dipole_hbm,
    occ_ref,
    orb_ref,
    ospin_ref,
    vspin_ref,
    out_ref,
    amps,
    dipole,
    commuted,
    masked,
    got_two,
    got_omega,
    got_commuted,
    got_masked,
    left,
    right,
    partial_sum,
    got_plane,
    slab,
    got_line,
    load_sem,
    own_sem,
    send_sem,
    recv_sem,
    plane_send,
    plane_recv,
    line_send,
    line_recv,
):
    pair = lax.axis_index("pair")
    virt = lax.axis_index("virt")
    me = pair * count_virt + virt
    count = count_pair * count_virt
    width = amps.shape[0]
    across = width // LANES

    load_amps = pltpu.make_async_copy(amps_hbm, amps, load_sem.at[0])
    load_dipole = pltpu.make_async_copy(dipole_hbm, dipole, load_sem.at[1])
    load_amps.start()
    load_dipole.start()

    def partner(step):
        return lax.rem(pair + step // count_virt, count_pair), lax.rem(virt + step, count_virt)

    barrier = pltpu.get_barrier_semaphore()

    @pl.loop(1, count)
    def _(step):
        pl.semaphore_signal(barrier, inc=1, device_id=partner(step), device_id_type=MESH)

    pl.semaphore_wait(barrier, count - 1)

    def tile(ref, owner):
        row = pl.multiple_of((owner // across) * ROWS, ROWS)
        col = pl.multiple_of((owner % across) * LANES, LANES)
        return ref.at[pl.ds(row, ROWS), pl.ds(col, LANES)]

    def slot(ref, owner):
        return ref.at[pl.ds(pl.multiple_of(owner * ROWS, ROWS), ROWS)]

    def send(which, source, target):
        pltpu.make_async_copy(tile(source, me), slot(target, me), own_sem.at[which]).start()

        @pl.loop(1, count)
        def _(step):
            to_pair, to_virt = partner(step)
            pltpu.make_async_remote_copy(
                src_ref=tile(source, to_pair * count_virt + to_virt),
                dst_ref=slot(target, me),
                send_sem=send_sem.at[which],
                recv_sem=recv_sem.at[which],
                device_id=(to_pair, to_virt),
                device_id_type=MESH,
            ).start()

    def all_of(which, target):
        rest = target.at[pl.ds(0, (count - 1) * ROWS)]
        return pltpu.make_async_remote_copy(
            src_ref=rest,
            dst_ref=rest,
            send_sem=send_sem.at[which],
            recv_sem=recv_sem.at[which],
            device_id=(pair, virt),
            device_id_type=MESH,
        )

    def arrived(which, source, target):
        pltpu.make_async_copy(tile(source, me), slot(target, me), own_sem.at[which]).wait()
        all_of(which, target).wait_recv()

    send(0, omega_hbm, got_omega)

    load_amps.wait()
    load_dipole.wait()
    first, second = orb_ref[0, 0], orb_ref[0, 1]
    shift = occ_ref[first] + occ_ref[second]
    target_spin = (ospin_ref[first] + ospin_ref[second]).astype(jnp.float32)
    spins = vspin_ref[...].astype(jnp.float32)

    @pl.loop(0, width // BLOCK)
    def _(block):
        at = pl.ds(pl.multiple_of(block * BLOCK, BLOCK), BLOCK)
        own = vspin_ref[:, at].astype(jnp.float32)
        column = jnp.broadcast_to(own, (BLOCK, BLOCK)).T[:, 0:1]
        allowed = (column + spins) == target_spin
        rows = amps[at, :]
        value = jnp.dot(dipole[at, :], amps[...], preferred_element_type=jnp.float32)
        value += lax.dot_general(
            rows, dipole[...], (((1,), (1,)), ((), ())), preferred_element_type=jnp.float32
        )
        wide = rows.astype(jnp.float32)
        value -= shift * wide
        commuted[at, :] = jnp.where(allowed, value, 0.0).astype(jnp.bfloat16)
        masked[at, :] = jnp.where(allowed, wide, 0.0).astype(jnp.bfloat16)

    send(1, masked, got_masked)
    send(2, two_hbm, got_two)
    send(3, commuted, got_commuted)

    size = GROUP * ROWS
    row_id = lax.broadcasted_iota(jnp.int32, (size, size), 0)
    col_id = lax.broadcasted_iota(jnp.int32, (size, size), 1)
    swap = (col_id == (row_id % GROUP) * ROWS + row_id // GROUP).astype(jnp.bfloat16)

    def regroup(got, into):
        @pl.loop(0, count // GROUP)
        def _(g):
            block = got[pl.ds(pl.multiple_of(g * size, size), size), :]
            moved = jnp.dot(swap, block, preferred_element_type=jnp.float32)
            into[:, pl.ds(pl.multiple_of(g * GROUP, GROUP), GROUP), :] = moved.reshape(
                ROWS, GROUP, LANES
            ).astype(jnp.bfloat16)

    def gram(first_time):
        if first_time:
            partial_sum[...] = jnp.zeros_like(partial_sum)

        @pl.loop(0, ROWS)
        def _(r):
            partial_sum[...] += lax.dot_general(
                left[r], right[r], (((1,), (1,)), ((), ())), preferred_element_type=jnp.float32
            )

    arrived(0, omega_hbm, got_omega)
    regroup(got_omega, left)
    arrived(1, masked, got_masked)
    regroup(got_masked, right)
    gram(True)
    arrived(2, two_hbm, got_two)
    regroup(got_two, left)
    arrived(3, commuted, got_commuted)
    regroup(got_commuted, right)
    gram(False)
    partial_sum[...] = partial_sum[...] * (1.0 / width)

    def strip(ref, owner):
        return ref.at[pl.ds(pl.multiple_of(owner * count_virt, count_virt), count_virt)]

    @pl.loop(1, count_pair)
    def _(step):
        to_pair = lax.rem(pair + step, count_pair)
        pltpu.make_async_remote_copy(
            src_ref=strip(partial_sum, to_pair),
            dst_ref=strip(got_plane, pair),
            send_sem=plane_send,
            recv_sem=plane_recv,
            device_id=(to_pair, virt),
            device_id_type=MESH,
        ).start()

    strip(got_plane, pair)[...] = strip(partial_sum, pair)[...]
    rest = got_plane.at[pl.ds(0, (count_pair - 1) * count_virt)]
    plane = pltpu.make_async_remote_copy(
        src_ref=rest,
        dst_ref=rest,
        send_sem=plane_send,
        recv_sem=plane_recv,
        device_id=(pair, virt),
        device_id_type=MESH,
    )
    plane.wait_recv()
    slab[...] = jnp.sum(got_plane[...].reshape(count_pair, count_virt, count), axis=0)

    lines = []
    for step in range(1, count_virt):
        to_virt = lax.rem(virt + step, count_virt)
        lines.append(
            pltpu.make_async_remote_copy(
                src_ref=slab,
                dst_ref=got_line.at[virt],
                send_sem=line_send,
                recv_sem=line_recv,
                device_id=(pair, to_virt),
                device_id_type=MESH,
            )
        )
        lines[-1].start()
    got_line[virt] = slab[...]
    rest_line = got_line.at[pl.ds(0, count_virt - 1)]
    line = pltpu.make_async_remote_copy(
        src_ref=rest_line,
        dst_ref=rest_line,
        send_sem=line_send,
        recv_sem=line_recv,
        device_id=(pair, virt),
        device_id_type=MESH,
    )
    line.wait_recv()
    total = got_line[0, pl.ds(virt, 1), :]
    for v in range(1, count_virt):
        total += got_line[v, pl.ds(virt, 1), :]
    out_ref[...] = total
    for which, target in enumerate((got_omega, got_masked, got_two, got_commuted)):
        all_of(which, target).wait_send()
    plane.wait_send()
    line.wait_send()


def solution(mesh):
    count_pair, count_virt = mesh.shape["pair"], mesh.shape["virt"]
    count = count_pair * count_virt

    def on_device(amps, two, omega, dipole, occ, orbitals, ospin, vspin):
        width = dipole.shape[0]
        half, full = jnp.bfloat16, jnp.float32
        vmem, smem, dma = pltpu.VMEM, pltpu.SMEM, pltpu.SemaphoreType.DMA
        return pl.pallas_call(
            functools.partial(kernel, count_pair, count_virt),
            out_shape=jax.ShapeDtypeStruct((1, count), full),
            in_specs=[pl.BlockSpec(memory_space=pl.ANY)] * 4
            + [pl.BlockSpec(memory_space=smem)] * 3
            + [pl.BlockSpec(memory_space=vmem)],
            out_specs=pl.BlockSpec(memory_space=vmem),
            scratch_shapes=[vmem((width, width), half)] * 4
            + [vmem((count * ROWS, LANES), half)] * 4
            + [vmem((ROWS, count, LANES), half)] * 2
            + [
                vmem((count, count), full),
                vmem((count, count), full),
                vmem((count_virt, count), full),
                vmem((count_virt, count_virt, count), full),
                dma((2,)),
                dma((4,)),
                dma((4,)),
                dma((4,)),
                dma,
                dma,
                dma,
                dma,
            ],
            compiler_params=pltpu.CompilerParams(
                collective_id=0, has_side_effects=True, vmem_limit_bytes=48 * 2**20
            ),
            name="response_gram",
        )(
            amps.reshape(width, width),
            two.reshape(width, width),
            omega.reshape(width, width),
            dipole,
            occ,
            orbitals,
            ospin,
            vspin.reshape(1, width),
        )

    rows = P(("pair", "virt"))
    return jax.shard_map(
        on_device,
        mesh=mesh,
        in_specs=(rows, rows, rows, P(), P(), rows, P(), P()),
        out_specs=P(("pair", "virt"), None),
        check_vma=False,
    )
```

```python
import functools

import jax
import jax.numpy as jnp
from jax import lax
from jax.experimental import pallas as pl
from jax.experimental.pallas import tpu as pltpu
from jax.sharding import PartitionSpec as P

MESH = pl.DeviceIdType.MESH
HALF, FULL = jnp.bfloat16, jnp.float32
ROWS, LANES = 16, 128
TILE = 2 * ROWS
BLOCK = 128
GROUP = 16
NARROW = 4
LAST = (((1,), (1,)), ((), ()))


def kernel(
    rings,
    count_virt,
    spill,
    amps_hbm,
    two_hbm,
    omega_hbm,
    dipole_hbm,
    occ_hbm,
    orb_hbm,
    ospin_hbm,
    vspin_hbm,
    out_ref,
    amps,
    dipole,
    omega,
    two,
    place,
    commuted,
    masked,
    put_omega,
    put_two,
    put_fold,
    put_spill,
    got_omega,
    got_two,
    got_fold,
    got_spill,
    left,
    right_masked,
    right_commuted,
    turned_masked,
    turned_commuted,
    partial_sum,
    ordered,
    got_plane,
    slab,
    got_line,
    occ,
    orb,
    ospin,
    vspin,
    own_target,
    plane_target,
    row_target,
    line_target,
    targets,
    load_sem,
    own_sem,
    send_sem,
    recv_sem,
    stage_send,
    stage_recv,
):
    pair = lax.axis_index("pair")
    virt = lax.axis_index("virt")
    count_pair = 2 * rings
    count = count_pair * count_virt
    me = pair * count_virt + virt
    width = amps.shape[0]
    strips = width // TILE
    blocks = width // BLOCK
    per_block = strips // blocks
    middle = width // 2

    loads = [
        pltpu.make_async_copy(source, into, load_sem.at[k])
        for k, (source, into) in enumerate(
            (
                (vspin_hbm, vspin),
                (omega_hbm, omega),
                (amps_hbm, amps),
                (dipole_hbm, dipole),
                (two_hbm, two),
                (occ_hbm, occ),
                (orb_hbm, orb),
                (ospin_hbm, ospin),
            )
        )
    ]
    for load in loads:
        load.start()

    def strip_of(p, v):
        ring, core = p // 2, p % 2
        turned = (v + ring) % count_virt
        spot = (turned % 4) * 4 + core * 2 + turned // 4
        return spot * 2 + ring // 8, ring % 8

    def owner_of(strip, column):
        spot, ring = strip // 2, (strip % 2) * 8 + column
        turned = (spot % 2) * 4 + spot // 4
        return ring * 2 + (spot // 2) % 2, (turned + count_virt * 2 - ring) % count_virt

    my_strip, my_column = strip_of(pair, virt)
    spills = my_strip >= strips - spill

    def tile(ref, strip, column):
        row = pl.multiple_of(strip * TILE, TILE)
        col = pl.multiple_of(column * LANES, LANES)
        return ref.at[pl.ds(row, TILE), pl.ds(col, LANES)]

    def slot(ref, owner):
        return ref.at[pl.ds(pl.multiple_of(owner * TILE, TILE), TILE)]

    def push(which, source, target, strip, column, base, here, sem):
        p, v = owner_of(strip, column)
        mine = p * count_virt + v == me

        @pl.when(mine)
        def _():
            pltpu.make_async_copy(
                tile(source, strip - base, column), slot(target, here), own_sem.at[which]
            ).start()

        @pl.when(jnp.logical_not(mine))
        def _():
            pltpu.make_async_remote_copy(
                src_ref=tile(source, strip - base, column),
                dst_ref=slot(target, here),
                send_sem=send_sem.at[which],
                recv_sem=recv_sem.at[sem],
                device_id=(p, v),
                device_id_type=MESH,
            ).start()

    def send(which, make, source, target, here, sem):
        @pl.loop(0, blocks)
        def _(k):
            block = lax.rem(k + virt, blocks)
            make(block)

            @pl.loop(0, per_block * 8)
            def _(i):
                j = lax.rem(i + 2 * (pair // 2), per_block * 8)
                push(
                    which,
                    source,
                    target,
                    block * per_block + (j % 2) * 2 + (j // 2) % 2,
                    j // 4,
                    0,
                    here,
                    sem,
                )

    def waiter(which, sem, target, copies):
        part = target.at[pl.ds(0, copies * TILE)]
        return pltpu.make_async_remote_copy(
            src_ref=part,
            dst_ref=part,
            send_sem=send_sem.at[which],
            recv_sem=recv_sem.at[sem],
            device_id=(pair, virt),
            device_id_type=MESH,
        )

    def own_arrived(which, source, target, base, here):
        pltpu.make_async_copy(
            tile(source, my_strip - base, my_column), slot(target, here), own_sem.at[which]
        ).wait()

    loads[0].wait()
    spins = vspin[...].astype(FULL)
    before = (
        lax.broadcasted_iota(jnp.int32, (BLOCK, BLOCK), 0)
        < lax.broadcasted_iota(jnp.int32, (BLOCK, BLOCK), 1)
    ).astype(FULL)
    ones_before = jnp.dot(spins, before, preferred_element_type=FULL)
    ones = jnp.zeros((1, 1), FULL)
    lane = lax.broadcasted_iota(jnp.int32, (1, BLOCK), 1)
    new_row = lax.broadcasted_iota(jnp.int32, (width, BLOCK), 0)
    for k in range(blocks):
        spin = spins[k : k + 1, :]
        up = (ones_before[k : k + 1, :] + ones).astype(jnp.int32)
        spin_up = spin.astype(jnp.int32)
        rank = jnp.where(spin_up == 1, up, lane + k * BLOCK - up)
        inside = rank < middle
        row = jnp.where(inside, rank, width - 1 - rank)
        bottom = jnp.where(inside, spin_up, 1 - spin_up)
        goal = row + (row & -ROWS) + bottom * ROWS
        place[:, k * BLOCK : (k + 1) * BLOCK] = jnp.where(new_row == goal, 1.0, 0.0).astype(HALF)
        ones += jnp.sum(spin, axis=1, keepdims=True)
    zeros = width - ones

    def permuted(block, source):
        at = pl.ds(pl.multiple_of(block * BLOCK, BLOCK), BLOCK)
        return jnp.dot(place[at, :], source[...], preferred_element_type=FULL), at

    def make_from(source, put):
        def make(block):
            moved, at = permuted(block, source)
            put[at, :] = moved.astype(HALF)

        return make

    loads[1].wait()
    turned_me = virt * count_pair + pair
    send(0, make_from(omega, put_omega), put_omega, got_omega, turned_me, 0)

    for load in loads[2:]:
        load.wait()
    first, second = orb[0, 0], orb[0, 1]
    shift = occ[first] + occ[second]
    target_spin = (ospin[first] + ospin[second]).astype(FULL)
    all_spins = jnp.concatenate([spins[k : k + 1, :] for k in range(blocks)], axis=1)

    @pl.loop(0, blocks)
    def _(block):
        at = pl.ds(pl.multiple_of(block * BLOCK, BLOCK), BLOCK)
        own = vspin[pl.ds(block, 1), :].astype(FULL)
        column = jnp.broadcast_to(own, (BLOCK, BLOCK)).T[:, 0:1]
        allowed = (column + all_spins) == target_spin
        rows = amps[at, :]
        value = jnp.dot(dipole[at, :], amps[...], preferred_element_type=FULL)
        value += lax.dot_general(rows, dipole[...], LAST, preferred_element_type=FULL)
        wide = rows.astype(FULL)
        value -= shift * wide
        commuted[at, :] = jnp.where(allowed, value, 0.0).astype(HALF)
        masked[at, :] = jnp.where(allowed, wide, 0.0).astype(HALF)

    def make_fold(block):
        row = (
            (block * per_block + lax.broadcasted_iota(jnp.int32, (per_block, ROWS, 1), 0)) * ROWS
            + lax.broadcasted_iota(jnp.int32, (per_block, ROWS, 1), 1)
        ).astype(FULL)
        top_in = row < zeros[:, :, None]
        bottom_in = row < ones[:, :, None]
        kept, over = [], []
        for source in (commuted, masked):
            moved, at = permuted(block, source)
            moved = moved.reshape(per_block, 2, ROWS, width)
            top, bottom = moved[:, 0], moved[:, 1]
            kept.append(jnp.where(top_in, top, 0.0) + jnp.where(bottom_in, bottom, 0.0))
            over.append(jnp.where(top_in, 0.0, top) + jnp.where(bottom_in, 0.0, bottom))
        put_fold[at, :] = jnp.stack(kept, axis=1).reshape(BLOCK, width).astype(HALF)
        first_spill = (strips - spill) // per_block

        @pl.when(block >= first_spill)
        def _():
            to = pl.ds(pl.multiple_of((block - first_spill) * BLOCK, BLOCK), BLOCK)
            put_spill[to, :] = jnp.stack(over, axis=1).reshape(BLOCK, width).astype(HALF)

    send(1, make_fold, put_fold, got_fold, me, 1)

    owners = spill * 8

    @pl.loop(0, owners)
    def _(i):
        j = lax.rem(i + me, owners)
        push(
            2, put_spill, got_spill, strips - spill + j // 8, j % 8, strips - spill, me, 2
        )

    send(3, make_from(two, put_two), put_two, got_two, turned_me, 3 + virt)

    def stage(which, copies, ref):
        part = ref.at[pl.ds(0, copies)]
        return pltpu.make_async_remote_copy(
            src_ref=part,
            dst_ref=part,
            send_sem=stage_send.at[which],
            recv_sem=stage_recv.at[which],
            device_id=(pair, virt),
            device_id_type=MESH,
        )

    own_target[...] = jnp.full((1, LANES), 1.0, FULL) * target_spin
    plane_target[pair] = own_target[...]

    @pl.loop(1, count_pair)
    def _(step):
        pltpu.make_async_remote_copy(
            src_ref=own_target,
            dst_ref=plane_target.at[pair],
            send_sem=stage_send.at[0],
            recv_sem=stage_recv.at[0],
            device_id=(lax.rem(pair + step, count_pair), virt),
            device_id_type=MESH,
        ).start()

    stage(0, count_pair - 1, plane_target).wait_recv()
    gathered = jnp.zeros((1, LANES), FULL)
    for p in range(count_pair):
        gathered = jnp.where(lane == p, plane_target[p], gathered)
    row_target[...] = gathered
    line_target[virt] = gathered
    for step in range(1, count_virt):
        pltpu.make_async_remote_copy(
            src_ref=row_target,
            dst_ref=line_target.at[virt],
            send_sem=stage_send.at[1],
            recv_sem=stage_recv.at[1],
            device_id=(pair, lax.rem(virt + step, count_virt)),
            device_id_type=MESH,
        ).start()
    stage(1, count_virt - 1, line_target).wait_recv()
    for v in range(count_virt):
        column = jnp.broadcast_to(line_target[v], (LANES, LANES)).T
        targets[pl.ds(v, count_pair, stride=count_virt), :] = column[0:count_pair]
    my_spins = vspin[pl.ds(my_column, 1), :].astype(FULL)

    size = GROUP * ROWS
    row_id = lax.broadcasted_iota(jnp.int32, (size, size), 0)
    col_id = lax.broadcasted_iota(jnp.int32, (size, size), 1)
    swap = (col_id == (row_id % GROUP) * ROWS + row_id // GROUP).astype(HALF)

    def regrouped(got, g):
        block = got[pl.ds(pl.multiple_of(g * GROUP * TILE, GROUP * TILE), GROUP * TILE), :]
        block = block.reshape(GROUP, 2, ROWS, LANES)
        wide = jnp.concatenate(
            [block[:, 0].reshape(size, LANES), block[:, 1].reshape(size, LANES)], axis=1
        )
        moved = jnp.dot(swap, wide, preferred_element_type=FULL)
        return moved.reshape(ROWS, GROUP, 2 * LANES)

    def regroup(got, into, g):
        at = pl.ds(pl.multiple_of(g * GROUP, GROUP), GROUP)
        moved = regrouped(got, g).astype(HALF)
        for r in range(ROWS):
            into[at, r * 2 * LANES : (r + 1) * 2 * LANES] = moved[r]

    def unfold(with_spill):
        @pl.loop(0, count // GROUP)
        def _(g):
            at = pl.ds(pl.multiple_of(g * GROUP, GROUP), GROUP)
            target = targets[at, :]
            top = (target == my_spins)[None]
            bottom = (target == my_spins + 1.0)[None]
            main = regrouped(got_fold, g)
            over = regrouped(got_spill, g) if with_spill else None
            for k, into in enumerate((right_commuted, right_masked)):
                half = main[:, :, k * LANES : (k + 1) * LANES]
                rest = over[:, :, k * LANES : (k + 1) * LANES] if with_spill else 0.0
                upper = jnp.where(top, half, jnp.where(bottom, rest, 0.0)).astype(HALF)
                lower = jnp.where(bottom, half, jnp.where(top, rest, 0.0)).astype(HALF)
                for r in range(ROWS):
                    into[at, 2 * r * LANES : (2 * r + 1) * LANES] = upper[r]
                    into[at, (2 * r + 1) * LANES : (2 * r + 2) * LANES] = lower[r]

        @pl.loop(0, ROWS)
        def _(r):
            at = pl.ds(pl.multiple_of(r * 2 * LANES, 2 * LANES), 2 * LANES)
            for flat, turned in ((right_commuted, turned_commuted), (right_masked, turned_masked)):
                turned[at, :] = flat[:, at].T

    own_arrived(0, put_omega, got_omega, 0, turned_me)
    waiter(0, 0, got_omega, count - 1).wait_recv()

    @pl.loop(0, count // GROUP)
    def _(g):
        regroup(got_omega, left, g)

    own_arrived(1, put_fold, got_fold, 0, me)
    waiter(1, 1, got_fold, count - 1).wait_recv()

    @pl.when(spills)
    def _():
        own_arrived(2, put_spill, got_spill, strips - spill, me)
        waiter(2, 2, got_spill, count - 1).wait_recv()
        unfold(True)

    @pl.when(jnp.logical_not(spills))
    def _():
        unfold(False)

    partial_sum[...] = jnp.dot(left[...], turned_masked[...], preferred_element_type=FULL)
    my_block = my_strip // per_block

    @pl.loop(0, count_virt)
    def _(k):
        v = lax.rem(my_block + count_virt - k, count_virt)

        @pl.when(v == virt)
        def _():
            own_arrived(3, put_two, got_two, 0, turned_me)
            waiter(3, 3 + v, got_two, count_pair - 1).wait_recv()

        @pl.when(v != virt)
        def _():
            waiter(3, 3 + v, got_two, count_pair).wait_recv()

        for half in range(count_pair // GROUP):
            regroup(got_two, left, v * (count_pair // GROUP) + half)

    partial_sum[...] = (
        partial_sum[...] + jnp.dot(left[...], turned_commuted[...], preferred_element_type=FULL)
    ) * (1.0 / width)
    for v in range(count_virt):
        for h in range(count // LANES):
            ordered[h, pl.ds(v, count_pair, stride=count_virt), :] = partial_sum[
                v * count_pair : (v + 1) * count_pair, h * LANES : (h + 1) * LANES
            ]

    def rows_of(ref, owner):
        return ref.at[:, pl.ds(pl.multiple_of(owner * count_virt, count_virt), count_virt)]

    for step in range(1, count_pair):
        to_pair = lax.rem(pair + step, count_pair)
        pltpu.make_async_remote_copy(
            src_ref=rows_of(ordered, to_pair),
            dst_ref=rows_of(got_plane, pair),
            send_sem=stage_send.at[2],
            recv_sem=stage_recv.at[2],
            device_id=(to_pair, virt),
            device_id_type=MESH,
        ).start()

    rows_of(got_plane, pair)[...] = rows_of(ordered, pair)[...]
    rest = got_plane.at[:, pl.ds(0, (count_pair - 1) * count_virt)]
    plane = pltpu.make_async_remote_copy(
        src_ref=rest,
        dst_ref=rest,
        send_sem=stage_send.at[2],
        recv_sem=stage_recv.at[2],
        device_id=(pair, virt),
        device_id_type=MESH,
    )
    plane.wait_recv()
    slab[...] = jnp.sum(
        got_plane[...].reshape(count // LANES, count_pair, count_virt, LANES), axis=1
    )

    for step in range(1, count_virt):
        pltpu.make_async_remote_copy(
            src_ref=slab,
            dst_ref=got_line.at[virt],
            send_sem=stage_send.at[3],
            recv_sem=stage_recv.at[3],
            device_id=(pair, lax.rem(virt + step, count_virt)),
            device_id_type=MESH,
        ).start()
    got_line[virt] = slab[...]
    line = stage(3, count_virt - 1, got_line)
    line.wait_recv()
    for h in range(count // LANES):
        total = got_line[0, h, pl.ds(virt, 1), :]
        for v in range(1, count_virt):
            total += got_line[v, h, pl.ds(virt, 1), :]
        out_ref[:, h * LANES : (h + 1) * LANES] = total
    for which, target in ((0, got_omega), (1, got_fold), (3, got_two)):
        waiter(which, which, target, count - 1).wait_send()

    @pl.when(spills)
    def _():
        waiter(2, 2, got_spill, owners - 1).wait_send()

    @pl.when(jnp.logical_not(spills))
    def _():
        waiter(2, 2, got_spill, owners).wait_send()

    stage(0, count_pair - 1, plane_target).wait_send()
    stage(1, count_virt - 1, line_target).wait_send()
    plane.wait_send()
    line.wait_send()


def solution(mesh):
    count_pair, count_virt = mesh.shape["pair"], mesh.shape["virt"]
    count = count_pair * count_virt

    def on_device(amps, two, omega, dipole, occ, orbitals, ospin, vspin):
        width = dipole.shape[0]
        vmem, smem, dma = pltpu.VMEM, pltpu.SMEM, pltpu.SemaphoreType.DMA

        def call(spill, name):
            square = vmem((width, width), HALF)
            got = vmem((count * TILE, LANES), HALF)
            flat = vmem((count, ROWS * 2 * LANES), HALF)
            turned = vmem((ROWS * 2 * LANES, count), HALF)
            return pl.pallas_call(
                functools.partial(kernel, count_pair // 2, count_virt, spill),
                out_shape=jax.ShapeDtypeStruct((1, count), FULL),
                in_specs=[pl.BlockSpec(memory_space=pltpu.HBM)] * 8,
                out_specs=pl.BlockSpec(memory_space=vmem),
                scratch_shapes=[square] * 10
                + [vmem((spill * TILE, width), HALF)]
                + [got] * 4
                + [flat] * 3
                + [turned] * 2
                + [
                    vmem((count, count), FULL),
                    vmem((count // LANES, count, LANES), FULL),
                    vmem((count // LANES, count, LANES), FULL),
                    vmem((count // LANES, count_virt, LANES), FULL),
                    vmem((count_virt, count // LANES, count_virt, LANES), FULL),
                    smem(occ.shape, occ.dtype),
                    smem(orbitals.shape, orbitals.dtype),
                    smem(ospin.shape, ospin.dtype),
                    vmem((width // LANES, LANES), vspin.dtype),
                    vmem((1, LANES), FULL),
                    vmem((count_pair, 1, LANES), FULL),
                    vmem((1, LANES), FULL),
                    vmem((count_virt, 1, LANES), FULL),
                    vmem((count, LANES), FULL),
                    dma((8,)),
                    dma((4,)),
                    dma((4,)),
                    dma((3 + count_virt,)),
                    dma((4,)),
                    dma((4,)),
                ],
                compiler_params=pltpu.CompilerParams(
                    has_side_effects=True, vmem_limit_bytes=60 * 2**20
                ),
                name=name,
            )

        arrays = (
            amps.reshape(width, width),
            two.reshape(width, width),
            omega.reshape(width, width),
            dipole,
            occ,
            orbitals,
            ospin,
            vspin.reshape(width // LANES, LANES),
        )
        ones = jnp.sum(vspin)
        reach = width // 2 + NARROW * ROWS
        return lax.cond(
            jnp.logical_and(ones <= reach, width - ones <= reach),
            call(NARROW, "folded_gram"),
            call(width // TILE, "whole_gram"),
            *arrays,
        )

    rows = P(("pair", "virt"))
    return jax.shard_map(
        on_device,
        mesh=mesh,
        in_specs=(rows, rows, rows, P(), P(), rows, P(), P()),
        out_specs=P(("pair", "virt"), None),
        check_vma=False,
    )
```

```python
import functools

import jax
import jax.numpy as jnp
from jax import lax
from jax.experimental import pallas as pl
from jax.experimental.pallas import tpu as pltpu
from jax.sharding import PartitionSpec as P

MESH = pl.DeviceIdType.MESH
HALF, FULL = jnp.bfloat16, jnp.float32
ROWS, LANES = 16, 128
TILE = 2 * ROWS
BLOCK = 128
GROUP = 16
NARROW = 4
LAST = (((1,), (1,)), ((), ()))


def kernel(
    rings,
    count_virt,
    spill,
    amps_hbm,
    two_hbm,
    omega_hbm,
    dipole_hbm,
    occ_hbm,
    orb_hbm,
    ospin_hbm,
    vspin_hbm,
    out_ref,
    amps,
    dipole,
    omega,
    two,
    place,
    commuted,
    masked,
    put_omega,
    put_two,
    put_fold,
    put_spill,
    got_omega,
    got_two,
    got_fold,
    got_spill,
    left_omega,
    left_two,
    right_masked,
    right_commuted,
    turned_masked,
    turned_commuted,
    partial_sum,
    got_plane,
    slab,
    got_line,
    occ,
    orb,
    ospin,
    vspin,
    own_target,
    plane_target,
    row_target,
    line_target,
    targets,
    load_sem,
    own_sem,
    send_sem,
    recv_sem,
    stage_send,
    stage_recv,
):
    pair = lax.axis_index("pair")
    virt = lax.axis_index("virt")
    count_pair = 2 * rings
    count = count_pair * count_virt
    me = pair * count_virt + virt
    width = amps.shape[0]
    strips = width // TILE
    blocks = width // BLOCK
    per_block = strips // blocks
    middle = width // 2

    loads = [
        pltpu.make_async_copy(source, into, load_sem.at[k])
        for k, (source, into) in enumerate(
            (
                (vspin_hbm, vspin),
                (omega_hbm, omega),
                (amps_hbm, amps),
                (dipole_hbm, dipole),
                (two_hbm, two),
                (occ_hbm, occ),
                (orb_hbm, orb),
                (ospin_hbm, ospin),
            )
        )
    ]
    for load in loads:
        load.start()

    def strip_of(p, v):
        ring, core = p // 2, p % 2
        turned = (v + ring) % count_virt
        spot = (turned % 4) * 4 + core * 2 + turned // 4
        return spot * 2 + ring // 8, ring % 8

    def owner_of(strip, column):
        spot, ring = strip // 2, (strip % 2) * 8 + column
        turned = (spot % 2) * 4 + spot // 4
        return ring * 2 + (spot // 2) % 2, (turned + count_virt * 2 - ring) % count_virt

    my_strip, my_column = strip_of(pair, virt)
    my_piece = pair // (count_pair // blocks)
    my_block = my_strip // per_block
    in_piece = count // blocks
    spills = my_strip >= strips - spill

    def tile(ref, strip, column):
        row = pl.multiple_of(strip * TILE, TILE)
        col = pl.multiple_of(column * LANES, LANES)
        return ref.at[pl.ds(row, TILE), pl.ds(col, LANES)]

    def slot(ref, owner):
        return ref.at[pl.ds(pl.multiple_of(owner * TILE, TILE), TILE)]

    def push(which, source, target, strip, column, base, sem):
        p, v = owner_of(strip, column)
        mine = p * count_virt + v == me

        @pl.when(mine)
        def _():
            pltpu.make_async_copy(
                tile(source, strip - base, column), slot(target, me), own_sem.at[which]
            ).start()

        @pl.when(jnp.logical_not(mine))
        def _():
            pltpu.make_async_remote_copy(
                src_ref=tile(source, strip - base, column),
                dst_ref=slot(target, me),
                send_sem=send_sem.at[which],
                recv_sem=recv_sem.at[sem],
                device_id=(p, v),
                device_id_type=MESH,
            ).start()

    def send(which, make, source, target, work):
        @pl.loop(0, blocks)
        def _(k):
            block = lax.rem(k + my_piece, blocks)
            make(block)

            @pl.loop(0, per_block * 8)
            def _(i):
                j = lax.rem(i + 2 * (pair // 2) + 4 * virt, per_block * 8)
                push(
                    which,
                    source,
                    target,
                    block * per_block + (j % 2) * 2 + (j // 2) % 2,
                    j // 4,
                    0,
                    which * blocks + my_piece,
                )

            work(k)

    def waiter(which, sem, target, copies):
        part = target.at[pl.ds(0, copies * TILE)]
        return pltpu.make_async_remote_copy(
            src_ref=part,
            dst_ref=part,
            send_sem=send_sem.at[which],
            recv_sem=recv_sem.at[sem],
            device_id=(pair, virt),
            device_id_type=MESH,
        )

    def own_arrived(which, source, target, base):
        pltpu.make_async_copy(
            tile(source, my_strip - base, my_column), slot(target, me), own_sem.at[which]
        ).wait()

    def piece_of(k):
        return lax.rem(my_block + blocks - k, blocks)

    def piece_arrived(which, source, target, piece):
        @pl.when(piece == my_piece)
        def _():
            own_arrived(which, source, target, 0)
            waiter(which, which * blocks + piece, target, in_piece - 1).wait_recv()

        @pl.when(piece != my_piece)
        def _():
            waiter(which, which * blocks + piece, target, in_piece).wait_recv()

    loads[0].wait()
    spins = vspin[...].astype(FULL)
    before = (
        lax.broadcasted_iota(jnp.int32, (BLOCK, BLOCK), 0)
        < lax.broadcasted_iota(jnp.int32, (BLOCK, BLOCK), 1)
    ).astype(FULL)
    ones_before = jnp.dot(spins, before, preferred_element_type=FULL)
    ones = jnp.zeros((1, 1), FULL)
    lane = lax.broadcasted_iota(jnp.int32, (1, BLOCK), 1)
    new_row = lax.broadcasted_iota(jnp.int32, (width, BLOCK), 0)
    for k in range(blocks):
        spin = spins[k : k + 1, :]
        up = (ones_before[k : k + 1, :] + ones).astype(jnp.int32)
        spin_up = spin.astype(jnp.int32)
        rank = jnp.where(spin_up == 1, up, lane + k * BLOCK - up)
        inside = rank < middle
        row = jnp.where(inside, rank, width - 1 - rank)
        bottom = jnp.where(inside, spin_up, 1 - spin_up)
        goal = row + (row & -ROWS) + bottom * ROWS
        place[:, k * BLOCK : (k + 1) * BLOCK] = jnp.where(new_row == goal, 1.0, 0.0).astype(HALF)
        ones += jnp.sum(spin, axis=1, keepdims=True)
    zeros = width - ones

    def permuted(block, source):
        at = pl.ds(pl.multiple_of(block * BLOCK, BLOCK), BLOCK)
        return jnp.dot(place[at, :], source[...], preferred_element_type=FULL), at

    def make_from(source, put):
        def make(block):
            moved, at = permuted(block, source)
            put[at, :] = moved.astype(HALF)

        return make

    loads[1].wait()
    send(0, make_from(omega, put_omega), put_omega, got_omega, lambda k: None)

    for load in loads[2:]:
        load.wait()
    first, second = orb[0, 0], orb[0, 1]
    shift = occ[first] + occ[second]
    target_spin = (ospin[first] + ospin[second]).astype(FULL)
    def stage(which, copies, ref):
        part = ref.at[pl.ds(0, copies)]
        return pltpu.make_async_remote_copy(
            src_ref=part,
            dst_ref=part,
            send_sem=stage_send.at[which],
            recv_sem=stage_recv.at[which],
            device_id=(pair, virt),
            device_id_type=MESH,
        )

    own_target[...] = jnp.full((1, LANES), 1.0, FULL) * target_spin
    plane_target[pair] = own_target[...]

    @pl.loop(1, count_pair)
    def _(step):
        pltpu.make_async_remote_copy(
            src_ref=own_target,
            dst_ref=plane_target.at[pair],
            send_sem=stage_send.at[0],
            recv_sem=stage_recv.at[0],
            device_id=(lax.rem(pair + step, count_pair), virt),
            device_id_type=MESH,
        ).start()

    all_spins = jnp.concatenate([spins[k : k + 1, :] for k in range(blocks)], axis=1)

    @pl.loop(0, blocks)
    def _(block):
        at = pl.ds(pl.multiple_of(block * BLOCK, BLOCK), BLOCK)
        own = vspin[pl.ds(block, 1), :].astype(FULL)
        column = jnp.broadcast_to(own, (BLOCK, BLOCK)).T[:, 0:1]
        allowed = (column + all_spins) == target_spin
        rows = amps[at, :]
        value = jnp.dot(dipole[at, :], amps[...], preferred_element_type=FULL)
        value += lax.dot_general(rows, dipole[...], LAST, preferred_element_type=FULL)
        wide = rows.astype(FULL)
        value -= shift * wide
        commuted[at, :] = jnp.where(allowed, value, 0.0).astype(HALF)
        masked[at, :] = jnp.where(allowed, wide, 0.0).astype(HALF)

    def make_fold(block):
        row = (
            (block * per_block + lax.broadcasted_iota(jnp.int32, (per_block, ROWS, 1), 0)) * ROWS
            + lax.broadcasted_iota(jnp.int32, (per_block, ROWS, 1), 1)
        ).astype(FULL)
        top_in = row < zeros[:, :, None]
        bottom_in = row < ones[:, :, None]
        kept, over = [], []
        for source in (commuted, masked):
            moved, at = permuted(block, source)
            moved = moved.reshape(per_block, 2, ROWS, width)
            top, bottom = moved[:, 0], moved[:, 1]
            kept.append(jnp.where(top_in, top, 0.0) + jnp.where(bottom_in, bottom, 0.0))
            over.append(jnp.where(top_in, 0.0, top) + jnp.where(bottom_in, 0.0, bottom))
        put_fold[at, :] = jnp.stack(kept, axis=1).reshape(BLOCK, width).astype(HALF)
        first_spill = (strips - spill) // per_block

        @pl.when(block >= first_spill)
        def _():
            to = pl.ds(pl.multiple_of((block - first_spill) * BLOCK, BLOCK), BLOCK)
            put_spill[to, :] = jnp.stack(over, axis=1).reshape(BLOCK, width).astype(HALF)

    @pl.loop(0, blocks)
    def _(block):
        make_fold(block)

    stage(0, count_pair - 1, plane_target).wait_recv()
    gathered = jnp.zeros((1, LANES), FULL)
    for p in range(count_pair):
        gathered = jnp.where(lane == p, plane_target[p], gathered)
    row_target[...] = gathered
    line_target[virt] = gathered
    for step in range(1, count_virt):
        pltpu.make_async_remote_copy(
            src_ref=row_target,
            dst_ref=line_target.at[virt],
            send_sem=stage_send.at[1],
            recv_sem=stage_recv.at[1],
            device_id=(pair, lax.rem(virt + step, count_virt)),
            device_id_type=MESH,
        ).start()
    owners = spill * 8

    @pl.loop(0, owners)
    def _(i):
        j = lax.rem(i + me, owners)
        push(
            2,
            put_spill,
            got_spill,
            strips - spill + j // 8,
            j % 8,
            strips - spill,
            2 * blocks,
        )

    size = GROUP * ROWS
    row_id = lax.broadcasted_iota(jnp.int32, (size, size), 0)
    col_id = lax.broadcasted_iota(jnp.int32, (size, size), 1)
    swap = (col_id == (row_id % GROUP) * ROWS + row_id // GROUP).astype(HALF)

    def regrouped(got, g):
        block = got[pl.ds(pl.multiple_of(g * GROUP * TILE, GROUP * TILE), GROUP * TILE), :]
        block = block.reshape(GROUP, 2, ROWS, LANES)
        wide = jnp.concatenate(
            [block[:, 0].reshape(size, LANES), block[:, 1].reshape(size, LANES)], axis=1
        )
        moved = jnp.dot(swap, wide, preferred_element_type=FULL)
        return moved.reshape(ROWS, GROUP, 2 * LANES)

    def regroup(got, into, k):
        for half in range(in_piece // GROUP):
            at = pl.ds(pl.multiple_of(k * in_piece + half * GROUP, GROUP), GROUP)
            moved = regrouped(got, piece_of(k) * (in_piece // GROUP) + half).astype(HALF)
            for r in range(ROWS):
                into[at, r * 2 * LANES : (r + 1) * 2 * LANES] = moved[r]

    def take_omega(k):
        piece_arrived(0, put_omega, got_omega, piece_of(k))
        regroup(got_omega, left_omega, k)

    send(1, lambda block: None, put_fold, got_fold, take_omega)

    stage(1, count_virt - 1, line_target).wait_recv()
    for v in range(count_virt):
        column = jnp.broadcast_to(line_target[v], (LANES, LANES)).T
        targets[pl.ds(v, count_pair, stride=count_virt), :] = column[0:count_pair]
    my_spins = vspin[pl.ds(my_column, 1), :].astype(FULL)

    @pl.when(spills)
    def _():
        own_arrived(2, put_spill, got_spill, strips - spill)
        waiter(2, 2 * blocks, got_spill, count - 1).wait_recv()

    def unfold(g, with_spill):
        at = pl.ds(pl.multiple_of(g * GROUP, GROUP), GROUP)
        target = targets[at, :]
        top = (target == my_spins)[None]
        bottom = (target == my_spins + 1.0)[None]
        main = regrouped(got_fold, g)
        over = regrouped(got_spill, g) if with_spill else None
        for c, into in enumerate((right_commuted, right_masked)):
            half = main[:, :, c * LANES : (c + 1) * LANES]
            rest = over[:, :, c * LANES : (c + 1) * LANES] if with_spill else 0.0
            upper = jnp.where(top, half, jnp.where(bottom, rest, 0.0)).astype(HALF)
            lower = jnp.where(bottom, half, jnp.where(top, rest, 0.0)).astype(HALF)
            for r in range(ROWS):
                into[at, 2 * r * LANES : (2 * r + 1) * LANES] = upper[r]
                into[at, (2 * r + 1) * LANES : (2 * r + 2) * LANES] = lower[r]

    def take_fold(k):
        piece = piece_of(k)
        piece_arrived(1, put_fold, got_fold, piece)
        first_group = piece * (in_piece // GROUP)

        @pl.when(spills)
        def _():
            for half in range(in_piece // GROUP):
                unfold(first_group + half, True)

        @pl.when(jnp.logical_not(spills))
        def _():
            for half in range(in_piece // GROUP):
                unfold(first_group + half, False)

    send(3, make_from(two, put_two), put_two, got_two, take_fold)

    @pl.loop(0, ROWS)
    def _(r):
        at = pl.ds(pl.multiple_of(r * 2 * LANES, 2 * LANES), 2 * LANES)
        for flat, turned in ((right_commuted, turned_commuted), (right_masked, turned_masked)):
            turned[at, :] = flat[:, at].T

    partial_sum[...] = jnp.dot(left_omega[...], turned_masked[...], preferred_element_type=FULL)

    pairs_in_piece = count_pair // blocks

    def rows_of(ref, owner):
        return ref.at[pl.ds(pl.multiple_of(owner * count_virt, count_virt), count_virt)]

    def give(k, u):
        to_pair = piece_of(k) * pairs_in_piece + u
        source = rows_of(partial_sum, k * pairs_in_piece + u)

        @pl.when(to_pair == pair)
        def _():
            rows_of(got_plane, pair)[...] = source[...]

        @pl.when(to_pair != pair)
        def _():
            pltpu.make_async_remote_copy(
                src_ref=source,
                dst_ref=rows_of(got_plane, pair),
                send_sem=stage_send.at[2],
                recv_sem=stage_recv.at[2],
                device_id=(to_pair, virt),
                device_id_type=MESH,
            ).start()

    for start, stop in ((0, blocks // 2), (blocks // 2, blocks - 1), (blocks - 1, blocks)):

        @pl.loop(start, stop)
        def _(k):
            piece_arrived(3, put_two, got_two, piece_of(k))
            regroup(got_two, left_two, k)

        at = slice(start * in_piece, stop * in_piece)
        partial_sum[at, :] = (
            partial_sum[at, :]
            + jnp.dot(left_two[at, :], turned_commuted[...], preferred_element_type=FULL)
        ) * (1.0 / width)
        for k in range(start, stop):
            for u in range(pairs_in_piece):
                give(k, u)

    plane = stage(2, (count_pair - 1) * count_virt, got_plane)
    plane.wait_recv()
    summed = jnp.sum(got_plane[...].reshape(count_pair, count_virt, count), axis=0)
    for v in range(count_virt):
        slab[v] = summed[v : v + 1, :]

    for step in range(1, count_virt):
        pltpu.make_async_remote_copy(
            src_ref=slab.at[lax.rem(virt + step, count_virt)],
            dst_ref=got_line.at[virt],
            send_sem=stage_send.at[3],
            recv_sem=stage_recv.at[3],
            device_id=(pair, lax.rem(virt + step, count_virt)),
            device_id_type=MESH,
        ).start()
    got_line[virt] = slab[virt]
    line = stage(3, count_virt - 1, got_line)
    line.wait_recv()
    total = got_line[0]
    for v in range(1, count_virt):
        total += got_line[v]
    out_ref[...] = total
    for which, target in ((0, got_omega), (1, got_fold), (3, got_two)):
        waiter(which, which * blocks, target, count - 1).wait_send()

    @pl.when(spills)
    def _():
        waiter(2, 2 * blocks, got_spill, owners - 1).wait_send()

    @pl.when(jnp.logical_not(spills))
    def _():
        waiter(2, 2 * blocks, got_spill, owners).wait_send()

    stage(0, count_pair - 1, plane_target).wait_send()
    stage(1, count_virt - 1, line_target).wait_send()
    plane.wait_send()
    line.wait_send()


def solution(mesh):
    count_pair, count_virt = mesh.shape["pair"], mesh.shape["virt"]
    count = count_pair * count_virt

    def on_device(amps, two, omega, dipole, occ, orbitals, ospin, vspin):
        width = dipole.shape[0]
        vmem, smem, dma = pltpu.VMEM, pltpu.SMEM, pltpu.SemaphoreType.DMA

        def call(spill, name):
            square = vmem((width, width), HALF)
            got = vmem((count * TILE, LANES), HALF)
            flat = vmem((count, ROWS * 2 * LANES), HALF)
            turned = vmem((ROWS * 2 * LANES, count), HALF)
            return pl.pallas_call(
                functools.partial(kernel, count_pair // 2, count_virt, spill),
                out_shape=jax.ShapeDtypeStruct((1, count), FULL),
                in_specs=[pl.BlockSpec(memory_space=pltpu.HBM)] * 8,
                out_specs=pl.BlockSpec(memory_space=vmem),
                scratch_shapes=[square] * 10
                + [vmem((spill * TILE, width), HALF)]
                + [got] * 4
                + [flat] * 4
                + [turned] * 2
                + [
                    vmem((count, count), FULL),
                    vmem((count, count), FULL),
                    vmem((count_virt, 1, count), FULL),
                    vmem((count_virt, 1, count), FULL),
                    smem(occ.shape, occ.dtype),
                    smem(orbitals.shape, orbitals.dtype),
                    smem(ospin.shape, ospin.dtype),
                    vmem((width // LANES, LANES), vspin.dtype),
                    vmem((1, LANES), FULL),
                    vmem((count_pair, 1, LANES), FULL),
                    vmem((1, LANES), FULL),
                    vmem((count_virt, 1, LANES), FULL),
                    vmem((count, LANES), FULL),
                    dma((8,)),
                    dma((4,)),
                    dma((4,)),
                    dma((4 * width // BLOCK,)),
                    dma((4,)),
                    dma((4,)),
                ],
                compiler_params=pltpu.CompilerParams(
                    has_side_effects=True, vmem_limit_bytes=60 * 2**20
                ),
                name=name,
            )

        arrays = (
            amps.reshape(width, width),
            two.reshape(width, width),
            omega.reshape(width, width),
            dipole,
            occ,
            orbitals,
            ospin,
            vspin.reshape(width // LANES, LANES),
        )
        ones = jnp.sum(vspin)
        reach = width // 2 + NARROW * ROWS
        return lax.cond(
            jnp.logical_and(ones <= reach, width - ones <= reach),
            call(NARROW, "folded_gram"),
            call(width // TILE, "whole_gram"),
            *arrays,
        )

    rows = P(("pair", "virt"))
    return jax.shard_map(
        on_device,
        mesh=mesh,
        in_specs=(rows, rows, rows, P(), P(), rows, P(), P()),
        out_specs=P(("pair", "virt"), None),
        check_vma=False,
    )
```

```python
import functools

import jax
import jax.numpy as jnp
from jax import lax
from jax.experimental import pallas as pl
from jax.experimental.pallas import tpu as pltpu
from jax.sharding import PartitionSpec as P

MESH = pl.DeviceIdType.MESH
HALF, FULL = jnp.bfloat16, jnp.float32
ROWS, LANES = 16, 128
TILE = 2 * ROWS
BLOCK = 128
GROUP = 16
NARROW = 4
LAST = (((1,), (1,)), ((), ()))


def kernel(
    rings,
    count_virt,
    spill,
    amps_hbm,
    two_hbm,
    omega_hbm,
    dipole_hbm,
    occ_hbm,
    orb_hbm,
    ospin_hbm,
    vspin_hbm,
    out_ref,
    flag_ref,
    amps,
    dipole,
    omega,
    two,
    place,
    commuted,
    masked,
    put_omega,
    put_two,
    put_fold,
    put_spill,
    got_omega,
    got_two,
    got_fold,
    got_spill,
    left_omega,
    left_two,
    right_masked,
    right_commuted,
    turned_masked,
    turned_commuted,
    partial_sum,
    got_plane,
    slab,
    got_line,
    occ,
    orb,
    ospin,
    vspin,
    own_target,
    plane_target,
    row_target,
    line_target,
    targets,
    load_sem,
    own_sem,
    send_sem,
    recv_sem,
    stage_send,
    stage_recv,
):
    pair = lax.axis_index("pair")
    virt = lax.axis_index("virt")
    count_pair = 2 * rings
    count = count_pair * count_virt
    me = pair * count_virt + virt
    width = amps.shape[0]
    strips = width // TILE
    blocks = width // BLOCK
    per_block = strips // blocks
    middle = width // 2

    loads = [
        pltpu.make_async_copy(source, into, load_sem.at[k])
        for k, (source, into) in enumerate(
            (
                (vspin_hbm, vspin),
                (omega_hbm, omega),
                (amps_hbm, amps),
                (dipole_hbm, dipole),
                (two_hbm, two),
                (occ_hbm, occ),
                (orb_hbm, orb),
                (ospin_hbm, ospin),
            )
        )
    ]
    for load in loads:
        load.start()

    def strip_of(p, v):
        ring, core = lax.div(p, 2), lax.rem(p, 2)
        turned = lax.rem(v + ring, count_virt)
        spot = lax.rem(turned, 4) * 4 + core * 2 + lax.div(turned, 4)
        return spot * 2 + lax.div(ring, 8), lax.rem(ring, 8)

    def owner_of(strip, column):
        spot, ring = lax.div(strip, 2), lax.rem(strip, 2) * 8 + column
        turned = lax.rem(spot, 2) * 4 + lax.div(spot, 4)
        return (
            ring * 2 + lax.rem(lax.div(spot, 2), 2),
            lax.rem(turned + count_virt * 2 - ring, count_virt),
        )

    my_strip, my_column = strip_of(pair, virt)
    my_piece = lax.div(pair, count_pair // blocks)
    my_block = lax.div(my_strip, per_block)
    in_piece = count // blocks
    spills = my_strip >= strips - spill

    def tile(ref, strip, column):
        row = pl.multiple_of(strip * TILE, TILE)
        col = pl.multiple_of(column * LANES, LANES)
        return ref.at[pl.ds(row, TILE), pl.ds(col, LANES)]

    def slot(ref, owner):
        return ref.at[pl.ds(pl.multiple_of(owner * TILE, TILE), TILE)]

    def push(which, source, target, strip, column, base, sem):
        p, v = owner_of(strip, column)
        mine = p * count_virt + v == me

        @pl.when(mine)
        def _():
            pltpu.make_async_copy(
                tile(source, strip - base, column), slot(target, me), own_sem.at[which]
            ).start()

        @pl.when(jnp.logical_not(mine))
        def _():
            pltpu.make_async_remote_copy(
                src_ref=tile(source, strip - base, column),
                dst_ref=slot(target, me),
                send_sem=send_sem.at[which],
                recv_sem=recv_sem.at[sem],
                device_id=(p, v),
                device_id_type=MESH,
            ).start()

    turn = lax.div(pair, 2) * 2 + virt * 4

    def send(which, make, source, target, work):
        @pl.loop(0, blocks)
        def _(k):
            block = lax.rem(k + my_piece, blocks)
            make(block)

            @pl.loop(0, per_block * 8)
            def _(i):
                j = lax.rem(i + turn, per_block * 8)
                push(
                    which,
                    source,
                    target,
                    block * per_block + lax.rem(j, 4),
                    lax.div(j, 4),
                    0,
                    which * blocks + my_piece,
                )

            work(k)

    def waiter(which, sem, target, copies):
        part = target.at[pl.ds(0, copies * TILE)]
        return pltpu.make_async_remote_copy(
            src_ref=part,
            dst_ref=part,
            send_sem=send_sem.at[which],
            recv_sem=recv_sem.at[sem],
            device_id=(pair, virt),
            device_id_type=MESH,
        )

    def own_arrived(which, source, target, base):
        pltpu.make_async_copy(
            tile(source, my_strip - base, my_column), slot(target, me), own_sem.at[which]
        ).wait()

    def piece_of(k):
        return lax.rem(my_block + blocks - k, blocks)

    def piece_arrived(which, source, target, piece):
        @pl.when(piece == my_piece)
        def _():
            own_arrived(which, source, target, 0)
            waiter(which, which * blocks + piece, target, in_piece - 1).wait_recv()

        @pl.when(piece != my_piece)
        def _():
            waiter(which, which * blocks + piece, target, in_piece).wait_recv()

    loads[0].wait()
    spins = vspin[...].astype(FULL)
    before = (
        lax.broadcasted_iota(jnp.int32, (BLOCK, BLOCK), 0)
        < lax.broadcasted_iota(jnp.int32, (BLOCK, BLOCK), 1)
    ).astype(FULL)
    ones_before = jnp.dot(spins, before, preferred_element_type=FULL)
    ones = jnp.zeros((1, 1), FULL)
    lane = lax.broadcasted_iota(jnp.int32, (1, BLOCK), 1)
    goals = []
    for k in range(blocks):
        spin = spins[k : k + 1, :]
        up = (ones_before[k : k + 1, :] + ones).astype(jnp.int32)
        spin_up = spin.astype(jnp.int32)
        rank = jnp.where(spin_up == 1, up, lane + k * BLOCK - up)
        inside = rank < middle
        row = jnp.where(inside, rank, width - 1 - rank)
        bottom = jnp.where(inside, spin_up, 1 - spin_up)
        goals.append(row + (row & -ROWS) + bottom * ROWS)
        ones += jnp.sum(spin, axis=1, keepdims=True)
    zeros = width - ones
    reach = middle + spill * ROWS
    most = jnp.max(jnp.maximum(ones, zeros))
    flag_ref[0, 0] = (most > reach).astype(jnp.int32)

    def make_place(block):
        at = pl.ds(pl.multiple_of(block * BLOCK, BLOCK), BLOCK)
        new_row = lax.broadcasted_iota(jnp.int32, (BLOCK, BLOCK), 0) + block * BLOCK
        for k in range(blocks):
            place[at, k * BLOCK : (k + 1) * BLOCK] = jnp.where(
                new_row == goals[k], 1.0, 0.0
            ).astype(HALF)

    def permuted(block, source):
        at = pl.ds(pl.multiple_of(block * BLOCK, BLOCK), BLOCK)
        return jnp.dot(place[at, :], source[...], preferred_element_type=FULL), at

    def make_from(source, put):
        def make(block):
            moved, at = permuted(block, source)
            put[at, :] = moved.astype(HALF)

        return make

    make_omega = make_from(omega, put_omega)

    def place_and_make(block):
        make_place(block)
        make_omega(block)

    loads[1].wait()
    send(0, place_and_make, put_omega, got_omega, lambda k: None)

    for load in loads[2:]:
        load.wait()
    first, second = orb[0, 0], orb[0, 1]
    shift = occ[first] + occ[second]
    target_spin = (ospin[first] + ospin[second]).astype(FULL)
    def stage(which, copies, ref):
        part = ref.at[pl.ds(0, copies)]
        return pltpu.make_async_remote_copy(
            src_ref=part,
            dst_ref=part,
            send_sem=stage_send.at[which],
            recv_sem=stage_recv.at[which],
            device_id=(pair, virt),
            device_id_type=MESH,
        )

    own_target[...] = jnp.full((1, LANES), 1.0, FULL) * target_spin
    plane_target[pair] = own_target[...]

    @pl.loop(1, count_pair)
    def _(step):
        pltpu.make_async_remote_copy(
            src_ref=own_target,
            dst_ref=plane_target.at[pair],
            send_sem=stage_send.at[0],
            recv_sem=stage_recv.at[0],
            device_id=(lax.rem(pair + step, count_pair), virt),
            device_id_type=MESH,
        ).start()

    all_spins = jnp.concatenate([spins[k : k + 1, :] for k in range(blocks)], axis=1)

    @pl.loop(0, blocks)
    def _(block):
        at = pl.ds(pl.multiple_of(block * BLOCK, BLOCK), BLOCK)
        own = vspin[pl.ds(block, 1), :].astype(FULL)
        column = jnp.broadcast_to(own, (BLOCK, BLOCK)).T[:, 0:1]
        allowed = (column + all_spins) == target_spin
        rows = amps[at, :]
        value = jnp.dot(dipole[at, :], amps[...], preferred_element_type=FULL)
        value += lax.dot_general(rows, dipole[...], LAST, preferred_element_type=FULL)
        wide = rows.astype(FULL)
        value -= shift * wide
        commuted[at, :] = jnp.where(allowed, value, 0.0).astype(HALF)
        masked[at, :] = jnp.where(allowed, wide, 0.0).astype(HALF)

    def make_fold(block):
        row = (
            (block * per_block + lax.broadcasted_iota(jnp.int32, (per_block, ROWS, 1), 0)) * ROWS
            + lax.broadcasted_iota(jnp.int32, (per_block, ROWS, 1), 1)
        ).astype(FULL)
        top_in = row < zeros[:, :, None]
        bottom_in = row < ones[:, :, None]
        kept, over = [], []
        for source in (commuted, masked):
            moved, at = permuted(block, source)
            moved = moved.reshape(per_block, 2, ROWS, width)
            top, bottom = moved[:, 0], moved[:, 1]
            kept.append(jnp.where(top_in, top, 0.0) + jnp.where(bottom_in, bottom, 0.0))
            over.append(jnp.where(top_in, 0.0, top) + jnp.where(bottom_in, 0.0, bottom))
        put_fold[at, :] = jnp.stack(kept, axis=1).reshape(BLOCK, width).astype(HALF)
        first_spill = (strips - spill) // per_block

        @pl.when(block >= first_spill)
        def _():
            to = pl.ds(pl.multiple_of((block - first_spill) * BLOCK, BLOCK), BLOCK)
            put_spill[to, :] = jnp.stack(over, axis=1).reshape(BLOCK, width).astype(HALF)

    @pl.loop(0, blocks)
    def _(block):
        make_fold(block)

    stage(0, count_pair - 1, plane_target).wait_recv()
    gathered = jnp.zeros((1, LANES), FULL)
    for p in range(count_pair):
        gathered = jnp.where(lane == p, plane_target[p], gathered)
    row_target[...] = gathered
    line_target[virt] = gathered
    for step in range(1, count_virt):
        pltpu.make_async_remote_copy(
            src_ref=row_target,
            dst_ref=line_target.at[virt],
            send_sem=stage_send.at[1],
            recv_sem=stage_recv.at[1],
            device_id=(pair, lax.rem(virt + step, count_virt)),
            device_id_type=MESH,
        ).start()
    owners = spill * 8

    @pl.loop(0, owners)
    def _(i):
        j = lax.rem(i + me, owners)
        push(
            2,
            put_spill,
            got_spill,
            strips - spill + lax.div(j, 8),
            lax.rem(j, 8),
            strips - spill,
            2 * blocks,
        )

    size = GROUP * ROWS
    row_id = lax.broadcasted_iota(jnp.int32, (size, size), 0)
    col_id = lax.broadcasted_iota(jnp.int32, (size, size), 1)
    swap = (col_id == (row_id % GROUP) * ROWS + row_id // GROUP).astype(HALF)

    def regrouped(got, g):
        block = got[pl.ds(pl.multiple_of(g * GROUP * TILE, GROUP * TILE), GROUP * TILE), :]
        block = block.reshape(GROUP, 2, ROWS, LANES)
        wide = jnp.concatenate(
            [block[:, 0].reshape(size, LANES), block[:, 1].reshape(size, LANES)], axis=1
        )
        moved = jnp.dot(swap, wide, preferred_element_type=FULL)
        return moved.reshape(ROWS, GROUP, 2 * LANES)

    def regroup(got, into, k):
        for half in range(in_piece // GROUP):
            at = pl.ds(pl.multiple_of(k * in_piece + half * GROUP, GROUP), GROUP)
            moved = regrouped(got, piece_of(k) * (in_piece // GROUP) + half).astype(HALF)
            for r in range(ROWS):
                into[at, r * 2 * LANES : (r + 1) * 2 * LANES] = moved[r]

    def take_omega(k):
        piece_arrived(0, put_omega, got_omega, piece_of(k))
        regroup(got_omega, left_omega, k)

    send(1, lambda block: None, put_fold, got_fold, take_omega)

    stage(1, count_virt - 1, line_target).wait_recv()
    for v in range(count_virt):
        column = jnp.broadcast_to(line_target[v], (LANES, LANES)).T
        targets[pl.ds(v, count_pair, stride=count_virt), :] = column[0:count_pair]
    my_spins = vspin[pl.ds(my_column, 1), :].astype(FULL)

    @pl.when(spills)
    def _():
        own_arrived(2, put_spill, got_spill, strips - spill)
        waiter(2, 2 * blocks, got_spill, count - 1).wait_recv()

    def unfold(g, with_spill):
        at = pl.ds(pl.multiple_of(g * GROUP, GROUP), GROUP)
        target = targets[at, :]
        top = (target == my_spins)[None]
        bottom = (target == my_spins + 1.0)[None]
        main = regrouped(got_fold, g)
        over = regrouped(got_spill, g) if with_spill else None
        for c, into in enumerate((right_commuted, right_masked)):
            half = main[:, :, c * LANES : (c + 1) * LANES]
            rest = over[:, :, c * LANES : (c + 1) * LANES] if with_spill else 0.0
            upper = jnp.where(top, half, jnp.where(bottom, rest, 0.0)).astype(HALF)
            lower = jnp.where(bottom, half, jnp.where(top, rest, 0.0)).astype(HALF)
            for r in range(ROWS):
                into[at, 2 * r * LANES : (2 * r + 1) * LANES] = upper[r]
                into[at, (2 * r + 1) * LANES : (2 * r + 2) * LANES] = lower[r]

    def take_fold(k):
        piece = piece_of(k)
        piece_arrived(1, put_fold, got_fold, piece)
        first_group = piece * (in_piece // GROUP)

        @pl.when(spills)
        def _():
            for half in range(in_piece // GROUP):
                unfold(first_group + half, True)

        @pl.when(jnp.logical_not(spills))
        def _():
            for half in range(in_piece // GROUP):
                unfold(first_group + half, False)

    send(3, make_from(two, put_two), put_two, got_two, take_fold)

    @pl.loop(0, ROWS)
    def _(r):
        at = pl.ds(pl.multiple_of(r * 2 * LANES, 2 * LANES), 2 * LANES)
        for flat, turned in ((right_commuted, turned_commuted), (right_masked, turned_masked)):
            turned[at, :] = flat[:, at].T

    partial_sum[...] = jnp.dot(left_omega[...], turned_masked[...], preferred_element_type=FULL)

    pairs_in_piece = count_pair // blocks

    def rows_of(ref, owner):
        return ref.at[pl.ds(pl.multiple_of(owner * count_virt, count_virt), count_virt)]

    def give(k, u):
        to_pair = piece_of(k) * pairs_in_piece + u
        source = rows_of(partial_sum, k * pairs_in_piece + u)

        @pl.when(to_pair == pair)
        def _():
            rows_of(got_plane, pair)[...] = source[...]

        @pl.when(to_pair != pair)
        def _():
            pltpu.make_async_remote_copy(
                src_ref=source,
                dst_ref=rows_of(got_plane, pair),
                send_sem=stage_send.at[2],
                recv_sem=stage_recv.at[2],
                device_id=(to_pair, virt),
                device_id_type=MESH,
            ).start()

    for start, stop in ((0, blocks // 2), (blocks // 2, blocks - 1), (blocks - 1, blocks)):

        @pl.loop(start, stop)
        def _(k):
            piece_arrived(3, put_two, got_two, piece_of(k))
            regroup(got_two, left_two, k)

        at = slice(start * in_piece, stop * in_piece)
        partial_sum[at, :] = (
            partial_sum[at, :]
            + jnp.dot(left_two[at, :], turned_commuted[...], preferred_element_type=FULL)
        ) * (1.0 / width)
        for k in range(start, stop):
            for u in range(pairs_in_piece):
                give(k, u)

    plane = stage(2, (count_pair - 1) * count_virt, got_plane)
    plane.wait_recv()
    summed = jnp.sum(got_plane[...].reshape(count_pair, count_virt, count), axis=0)
    for v in range(count_virt):
        slab[v] = summed[v : v + 1, :]

    for step in range(1, count_virt):
        pltpu.make_async_remote_copy(
            src_ref=slab.at[lax.rem(virt + step, count_virt)],
            dst_ref=got_line.at[virt],
            send_sem=stage_send.at[3],
            recv_sem=stage_recv.at[3],
            device_id=(pair, lax.rem(virt + step, count_virt)),
            device_id_type=MESH,
        ).start()
    got_line[virt] = slab[virt]
    line = stage(3, count_virt - 1, got_line)
    line.wait_recv()
    total = got_line[0]
    for v in range(1, count_virt):
        total += got_line[v]
    out_ref[...] = total
    for which, target in ((0, got_omega), (1, got_fold), (3, got_two)):
        waiter(which, which * blocks, target, count - 1).wait_send()

    @pl.when(spills)
    def _():
        waiter(2, 2 * blocks, got_spill, owners - 1).wait_send()

    @pl.when(jnp.logical_not(spills))
    def _():
        waiter(2, 2 * blocks, got_spill, owners).wait_send()

    stage(0, count_pair - 1, plane_target).wait_send()
    stage(1, count_virt - 1, line_target).wait_send()
    plane.wait_send()
    line.wait_send()


def solution(mesh):
    count_pair, count_virt = mesh.shape["pair"], mesh.shape["virt"]
    count = count_pair * count_virt

    def on_device(amps, two, omega, dipole, occ, orbitals, ospin, vspin):
        width = dipole.shape[0]
        vmem, smem, dma = pltpu.VMEM, pltpu.SMEM, pltpu.SemaphoreType.DMA

        def call(spill, name):
            square = vmem((width, width), HALF)
            got = vmem((count * TILE, LANES), HALF)
            flat = vmem((count, ROWS * 2 * LANES), HALF)
            turned = vmem((ROWS * 2 * LANES, count), HALF)
            return pl.pallas_call(
                functools.partial(kernel, count_pair // 2, count_virt, spill),
                out_shape=(
                    jax.ShapeDtypeStruct((1, count), FULL),
                    jax.ShapeDtypeStruct((1, 1), jnp.int32),
                ),
                in_specs=[pl.BlockSpec(memory_space=pltpu.HBM)] * 8,
                out_specs=(pl.BlockSpec(memory_space=vmem), pl.BlockSpec(memory_space=smem)),
                scratch_shapes=[square] * 10
                + [vmem((spill * TILE, width), HALF)]
                + [got] * 4
                + [flat] * 4
                + [turned] * 2
                + [
                    vmem((count, count), FULL),
                    vmem((count, count), FULL),
                    vmem((count_virt, 1, count), FULL),
                    vmem((count_virt, 1, count), FULL),
                    smem(occ.shape, occ.dtype),
                    smem(orbitals.shape, orbitals.dtype),
                    smem(ospin.shape, ospin.dtype),
                    vmem((width // LANES, LANES), vspin.dtype),
                    vmem((1, LANES), FULL),
                    vmem((count_pair, 1, LANES), FULL),
                    vmem((1, LANES), FULL),
                    vmem((count_virt, 1, LANES), FULL),
                    vmem((count, LANES), FULL),
                    dma((8,)),
                    dma((4,)),
                    dma((4,)),
                    dma((4 * width // BLOCK,)),
                    dma((4,)),
                    dma((4,)),
                ],
                compiler_params=pltpu.CompilerParams(
                    has_side_effects=True, vmem_limit_bytes=60 * 2**20
                ),
                name=name,
            )

        arrays = (
            amps.reshape(width, width),
            two.reshape(width, width),
            omega.reshape(width, width),
            dipole,
            occ,
            orbitals,
            ospin,
            vspin.reshape(width // LANES, LANES),
        )
        gram, over = call(NARROW, "folded_gram")(*arrays)
        return lax.cond(
            over[0, 0] > 0, lambda _: call(width // TILE, "whole_gram")(*arrays)[0], lambda g: g, gram
        )

    rows = P(("pair", "virt"))
    return jax.shard_map(
        on_device,
        mesh=mesh,
        in_specs=(rows, rows, rows, P(), P(), rows, P(), P()),
        out_specs=P(("pair", "virt"), None),
        check_vma=False,
    )
```

```python
import functools

import jax
import jax.numpy as jnp
from jax import lax
from jax.experimental import pallas as pl
from jax.experimental.pallas import tpu as pltpu
from jax.sharding import PartitionSpec as P

MESH = pl.DeviceIdType.MESH
HALF, FULL = jnp.bfloat16, jnp.float32
ROWS, LANES = 16, 128
TILE = 2 * ROWS
BLOCK = 128
GROUP = 16
NARROW = 4
LAST = (((1,), (1,)), ((), ()))


def kernel(
    rings,
    count_virt,
    spill,
    amps_hbm,
    two_hbm,
    omega_hbm,
    dipole_hbm,
    occ_hbm,
    orb_hbm,
    ospin_hbm,
    vspin_hbm,
    out_ref,
    flag_ref,
    amps,
    dipole,
    omega,
    two,
    place,
    commuted,
    masked,
    put_omega,
    put_two,
    put_fold,
    put_spill,
    got_omega,
    got_two,
    got_fold,
    got_spill,
    left_omega,
    left_two,
    right_masked,
    right_commuted,
    turned_masked,
    turned_commuted,
    partial_sum,
    got_plane,
    slab,
    got_line,
    put_rows,
    got_rows,
    occ,
    orb,
    ospin,
    vspin,
    own_target,
    plane_target,
    row_target,
    line_target,
    targets,
    load_sem,
    own_sem,
    send_sem,
    recv_sem,
    stage_send,
    stage_recv,
):
    pair = lax.axis_index("pair")
    virt = lax.axis_index("virt")
    count_pair = 2 * rings
    count = count_pair * count_virt
    me = pair * count_virt + virt
    width = amps.shape[0]
    strips = width // TILE
    blocks = width // BLOCK
    per_block = strips // blocks
    middle = width // 2

    loads = [
        pltpu.make_async_copy(source, into, load_sem.at[k])
        for k, (source, into) in enumerate(
            (
                (vspin_hbm, vspin),
                (omega_hbm, omega),
                (amps_hbm, amps),
                (dipole_hbm, dipole),
                (two_hbm, two),
                (occ_hbm, occ),
                (orb_hbm, orb),
                (ospin_hbm, ospin),
            )
        )
    ]
    for load in loads:
        load.start()

    def strip_of(p, v):
        ring, core = lax.div(p, 2), lax.rem(p, 2)
        turned = lax.rem(v + ring, count_virt)
        spot = lax.rem(turned, 4) * 4 + core * 2 + lax.div(turned, 4)
        return spot * 2 + lax.div(ring, 8), lax.rem(ring, 8)

    def owner_of(strip, column):
        spot, ring = lax.div(strip, 2), lax.rem(strip, 2) * 8 + column
        turned = lax.rem(spot, 2) * 4 + lax.div(spot, 4)
        return (
            ring * 2 + lax.rem(lax.div(spot, 2), 2),
            lax.rem(turned + count_virt * 2 - ring, count_virt),
        )

    my_strip, my_column = strip_of(pair, virt)
    my_piece = lax.div(pair, count_pair // blocks)
    my_block = lax.div(my_strip, per_block)
    in_piece = count // blocks
    spills = my_strip >= strips - spill

    def tile(ref, strip, column):
        row = pl.multiple_of(strip * TILE, TILE)
        col = pl.multiple_of(column * LANES, LANES)
        return ref.at[pl.ds(row, TILE), pl.ds(col, LANES)]

    def slot(ref, owner):
        return ref.at[pl.ds(pl.multiple_of(owner * TILE, TILE), TILE)]

    def push(which, source, target, strip, column, base, sem):
        p, v = owner_of(strip, column)
        mine = p * count_virt + v == me

        @pl.when(mine)
        def _():
            pltpu.make_async_copy(
                tile(source, strip - base, column), slot(target, me), own_sem.at[which]
            ).start()

        @pl.when(jnp.logical_not(mine))
        def _():
            pltpu.make_async_remote_copy(
                src_ref=tile(source, strip - base, column),
                dst_ref=slot(target, me),
                send_sem=send_sem.at[which],
                recv_sem=recv_sem.at[sem],
                device_id=(p, v),
                device_id_type=MESH,
            ).start()

    turn = lax.div(pair, 2) * 2 + virt * 4

    def send(which, make, source, target, work):
        @pl.loop(0, blocks)
        def _(k):
            block = lax.rem(k + my_piece, blocks)
            make(block)

            @pl.loop(0, per_block * 8)
            def _(i):
                j = lax.rem(i + turn, per_block * 8)
                push(
                    which,
                    source,
                    target,
                    block * per_block + lax.rem(j, 4),
                    lax.div(j, 4),
                    0,
                    which * blocks + my_piece,
                )

            work(k)

    def waiter(which, sem, target, copies):
        part = target.at[pl.ds(0, copies * TILE)]
        return pltpu.make_async_remote_copy(
            src_ref=part,
            dst_ref=part,
            send_sem=send_sem.at[which],
            recv_sem=recv_sem.at[sem],
            device_id=(pair, virt),
            device_id_type=MESH,
        )

    def own_arrived(which, source, target, base):
        pltpu.make_async_copy(
            tile(source, my_strip - base, my_column), slot(target, me), own_sem.at[which]
        ).wait()

    def piece_of(k):
        return lax.rem(my_block + blocks - k, blocks)

    def piece_arrived(which, source, target, piece):
        @pl.when(piece == my_piece)
        def _():
            own_arrived(which, source, target, 0)
            waiter(which, which * blocks + piece, target, in_piece - 1).wait_recv()

        @pl.when(piece != my_piece)
        def _():
            waiter(which, which * blocks + piece, target, in_piece).wait_recv()

    got_plane[...] = jnp.zeros_like(got_plane)
    loads[0].wait()
    spins = vspin[...].astype(FULL)
    before = (
        lax.broadcasted_iota(jnp.int32, (BLOCK, BLOCK), 0)
        < lax.broadcasted_iota(jnp.int32, (BLOCK, BLOCK), 1)
    ).astype(FULL)
    ones_before = jnp.dot(spins, before, preferred_element_type=FULL)
    ones = jnp.zeros((1, 1), FULL)
    lane = lax.broadcasted_iota(jnp.int32, (1, BLOCK), 1)
    goals = []
    for k in range(blocks):
        spin = spins[k : k + 1, :]
        up = (ones_before[k : k + 1, :] + ones).astype(jnp.int32)
        spin_up = spin.astype(jnp.int32)
        rank = jnp.where(spin_up == 1, up, lane + k * BLOCK - up)
        inside = rank < middle
        row = jnp.where(inside, rank, width - 1 - rank)
        bottom = jnp.where(inside, spin_up, 1 - spin_up)
        goals.append(row + (row & -ROWS) + bottom * ROWS)
        ones += jnp.sum(spin, axis=1, keepdims=True)
    zeros = width - ones
    reach = middle + spill * ROWS
    most = jnp.max(jnp.maximum(ones, zeros))
    flag_ref[0, 0] = (most > reach).astype(jnp.int32)

    def make_place(block):
        at = pl.ds(pl.multiple_of(block * BLOCK, BLOCK), BLOCK)
        new_row = lax.broadcasted_iota(jnp.int32, (BLOCK, BLOCK), 0) + block * BLOCK
        for k in range(blocks):
            place[at, k * BLOCK : (k + 1) * BLOCK] = jnp.where(
                new_row == goals[k], 1.0, 0.0
            ).astype(HALF)

    def permuted(block, source):
        at = pl.ds(pl.multiple_of(block * BLOCK, BLOCK), BLOCK)
        return jnp.dot(place[at, :], source[...], preferred_element_type=FULL), at

    def make_from(source, put):
        def make(block):
            moved, at = permuted(block, source)
            put[at, :] = moved.astype(HALF)

        return make

    make_omega = make_from(omega, put_omega)

    def place_and_make(block):
        make_place(block)
        make_omega(block)

    loads[1].wait()
    send(0, place_and_make, put_omega, got_omega, lambda k: None)

    for load in loads[2:]:
        load.wait()
    first, second = orb[0, 0], orb[0, 1]
    shift = occ[first] + occ[second]
    target_spin = (ospin[first] + ospin[second]).astype(FULL)
    def stage(which, copies, ref):
        part = ref.at[pl.ds(0, copies)]
        return pltpu.make_async_remote_copy(
            src_ref=part,
            dst_ref=part,
            send_sem=stage_send.at[which],
            recv_sem=stage_recv.at[which],
            device_id=(pair, virt),
            device_id_type=MESH,
        )

    own_target[...] = jnp.full((1, LANES), 1.0, FULL) * target_spin
    plane_target[pair] = own_target[...]

    @pl.loop(1, count_pair)
    def _(step):
        pltpu.make_async_remote_copy(
            src_ref=own_target,
            dst_ref=plane_target.at[pair],
            send_sem=stage_send.at[0],
            recv_sem=stage_recv.at[0],
            device_id=(lax.rem(pair + step, count_pair), virt),
            device_id_type=MESH,
        ).start()

    all_spins = jnp.concatenate([spins[k : k + 1, :] for k in range(blocks)], axis=1)

    @pl.loop(0, blocks)
    def _(block):
        at = pl.ds(pl.multiple_of(block * BLOCK, BLOCK), BLOCK)
        own = vspin[pl.ds(block, 1), :].astype(FULL)
        column = jnp.broadcast_to(own, (BLOCK, BLOCK)).T[:, 0:1]
        allowed = (column + all_spins) == target_spin
        rows = amps[at, :]
        value = jnp.dot(dipole[at, :], amps[...], preferred_element_type=FULL)
        value += lax.dot_general(rows, dipole[...], LAST, preferred_element_type=FULL)
        wide = rows.astype(FULL)
        value -= shift * wide
        commuted[at, :] = jnp.where(allowed, value, 0.0).astype(HALF)
        masked[at, :] = jnp.where(allowed, wide, 0.0).astype(HALF)

    def make_fold(block):
        row = (
            (block * per_block + lax.broadcasted_iota(jnp.int32, (per_block, ROWS, 1), 0)) * ROWS
            + lax.broadcasted_iota(jnp.int32, (per_block, ROWS, 1), 1)
        ).astype(FULL)
        top_in = row < zeros[:, :, None]
        bottom_in = row < ones[:, :, None]
        kept, over = [], []
        for source in (commuted, masked):
            moved, at = permuted(block, source)
            moved = moved.reshape(per_block, 2, ROWS, width)
            top, bottom = moved[:, 0], moved[:, 1]
            kept.append(jnp.where(top_in, top, 0.0) + jnp.where(bottom_in, bottom, 0.0))
            over.append(jnp.where(top_in, 0.0, top) + jnp.where(bottom_in, 0.0, bottom))
        put_fold[at, :] = jnp.stack(kept, axis=1).reshape(BLOCK, width).astype(HALF)
        first_spill = (strips - spill) // per_block

        @pl.when(block >= first_spill)
        def _():
            to = pl.ds(pl.multiple_of((block - first_spill) * BLOCK, BLOCK), BLOCK)
            put_spill[to, :] = jnp.stack(over, axis=1).reshape(BLOCK, width).astype(HALF)

    @pl.loop(0, blocks)
    def _(block):
        make_fold(block)

    stage(0, count_pair - 1, plane_target).wait_recv()
    gathered = jnp.zeros((1, LANES), FULL)
    for p in range(count_pair):
        gathered = jnp.where(lane == p, plane_target[p], gathered)
    row_target[...] = gathered
    line_target[virt] = gathered
    for step in range(1, count_virt):
        pltpu.make_async_remote_copy(
            src_ref=row_target,
            dst_ref=line_target.at[virt],
            send_sem=stage_send.at[1],
            recv_sem=stage_recv.at[1],
            device_id=(pair, lax.rem(virt + step, count_virt)),
            device_id_type=MESH,
        ).start()
    owners = spill * 8

    @pl.loop(0, owners)
    def _(i):
        j = lax.rem(i + me, owners)
        push(
            2,
            put_spill,
            got_spill,
            strips - spill + lax.div(j, 8),
            lax.rem(j, 8),
            strips - spill,
            2 * blocks,
        )

    size = GROUP * ROWS
    row_id = lax.broadcasted_iota(jnp.int32, (size, size), 0)
    col_id = lax.broadcasted_iota(jnp.int32, (size, size), 1)
    swap = (col_id == (row_id % GROUP) * ROWS + row_id // GROUP).astype(HALF)

    def regrouped(got, g):
        block = got[pl.ds(pl.multiple_of(g * GROUP * TILE, GROUP * TILE), GROUP * TILE), :]
        block = block.reshape(GROUP, 2, ROWS, LANES)
        wide = jnp.concatenate(
            [block[:, 0].reshape(size, LANES), block[:, 1].reshape(size, LANES)], axis=1
        )
        moved = jnp.dot(swap, wide, preferred_element_type=FULL)
        return moved.reshape(ROWS, GROUP, 2 * LANES)

    def regroup(got, into, k):
        for half in range(in_piece // GROUP):
            at = pl.ds(pl.multiple_of(k * in_piece + half * GROUP, GROUP), GROUP)
            moved = regrouped(got, piece_of(k) * (in_piece // GROUP) + half).astype(HALF)
            for r in range(ROWS):
                into[at, r * 2 * LANES : (r + 1) * 2 * LANES] = moved[r]

    def take_omega(k):
        piece_arrived(0, put_omega, got_omega, piece_of(k))
        regroup(got_omega, left_omega, k)

    send(1, lambda block: None, put_fold, got_fold, take_omega)

    stage(1, count_virt - 1, line_target).wait_recv()
    for v in range(count_virt):
        column = jnp.broadcast_to(line_target[v], (LANES, LANES)).T
        targets[pl.ds(v, count_pair, stride=count_virt), :] = column[0:count_pair]
    my_spins = vspin[pl.ds(my_column, 1), :].astype(FULL)

    @pl.when(spills)
    def _():
        own_arrived(2, put_spill, got_spill, strips - spill)
        waiter(2, 2 * blocks, got_spill, count - 1).wait_recv()

    def unfold(g, with_spill):
        at = pl.ds(pl.multiple_of(g * GROUP, GROUP), GROUP)
        target = targets[at, :]
        top = (target == my_spins)[None]
        bottom = (target == my_spins + 1.0)[None]
        main = regrouped(got_fold, g)
        over = regrouped(got_spill, g) if with_spill else None
        for c, into in enumerate((right_commuted, right_masked)):
            half = main[:, :, c * LANES : (c + 1) * LANES]
            rest = over[:, :, c * LANES : (c + 1) * LANES] if with_spill else 0.0
            upper = jnp.where(top, half, jnp.where(bottom, rest, 0.0)).astype(HALF)
            lower = jnp.where(bottom, half, jnp.where(top, rest, 0.0)).astype(HALF)
            for r in range(ROWS):
                into[at, 2 * r * LANES : (2 * r + 1) * LANES] = upper[r]
                into[at, (2 * r + 1) * LANES : (2 * r + 2) * LANES] = lower[r]

    def take_fold(k):
        piece = piece_of(k)
        piece_arrived(1, put_fold, got_fold, piece)
        first_group = piece * (in_piece // GROUP)

        @pl.when(spills)
        def _():
            for half in range(in_piece // GROUP):
                unfold(first_group + half, True)

        @pl.when(jnp.logical_not(spills))
        def _():
            for half in range(in_piece // GROUP):
                unfold(first_group + half, False)

    send(3, make_from(two, put_two), put_two, got_two, take_fold)

    @pl.loop(0, ROWS)
    def _(r):
        at = pl.ds(pl.multiple_of(r * 2 * LANES, 2 * LANES), 2 * LANES)
        for flat, turned in ((right_commuted, turned_commuted), (right_masked, turned_masked)):
            turned[at, :] = flat[:, at].T

    partial_sum[...] = jnp.dot(left_omega[...], turned_masked[...], preferred_element_type=FULL)

    pairs_in_piece = count_pair // blocks

    def rows_of(ref, owner):
        return ref.at[pl.ds(pl.multiple_of(owner * count_virt, count_virt), count_virt)]

    def give(k, u):
        to_pair = piece_of(k) * pairs_in_piece + u
        source = rows_of(partial_sum, k * pairs_in_piece + u)

        @pl.when(to_pair == pair)
        def _():
            rows_of(got_plane, pair)[...] = source[...]

        @pl.when(to_pair != pair)
        def _():
            pltpu.make_async_remote_copy(
                src_ref=source,
                dst_ref=rows_of(got_plane, pair),
                send_sem=stage_send.at[2],
                recv_sem=stage_recv.at[2],
                device_id=(to_pair, virt),
                device_id_type=MESH,
            ).start()

    last = blocks - 1
    for start, stop in ((0, blocks // 2), (blocks // 2, last), (last, blocks)):

        @pl.loop(start, stop)
        def _(k):
            piece_arrived(3, put_two, got_two, piece_of(k))
            regroup(got_two, left_two, k)

        at = slice(start * in_piece, stop * in_piece)
        partial_sum[at, :] = (
            partial_sum[at, :]
            + jnp.dot(left_two[at, :], turned_commuted[...], preferred_element_type=FULL)
        ) * (1.0 / width)
        if start < last:
            for k in range(start, stop):
                for u in range(pairs_in_piece):
                    give(k, u)
        else:
            for i in range(in_piece):
                put_rows[i] = partial_sum[start * in_piece + i : start * in_piece + i + 1, :]

    my_row = lax.rem(my_strip, per_block) * 8 + my_column
    first_pair = piece_of(last) * pairs_in_piece

    @pl.loop(0, in_piece)
    def _(step):
        i = lax.rem(step + my_row, in_piece)
        to_pair, to_virt = first_pair + lax.div(i, count_virt), lax.rem(i, count_virt)
        mine = to_pair * count_virt + to_virt == me

        @pl.when(mine)
        def _():
            got_rows[my_row] = put_rows[i]

        @pl.when(jnp.logical_not(mine))
        def _():
            pltpu.make_async_remote_copy(
                src_ref=put_rows.at[i],
                dst_ref=got_rows.at[my_row],
                send_sem=stage_send.at[4],
                recv_sem=stage_recv.at[4],
                device_id=(to_pair, to_virt),
                device_id_type=MESH,
            ).start()

    straight = piece_of(last) == my_piece
    strips_sent = (count_pair - pairs_in_piece) * count_virt

    def for_each(work):
        @pl.when(straight)
        def _():
            work(strips_sent, in_piece - 1)

        @pl.when(jnp.logical_not(straight))
        def _():
            work(strips_sent - count_virt, in_piece)

    for_each(lambda strips_in, _: stage(2, strips_in, got_plane).wait_recv())
    summed = jnp.sum(got_plane[...].reshape(count_pair, count_virt, count), axis=0)
    for v in range(count_virt):
        slab[v] = summed[v : v + 1, :]

    for step in range(1, count_virt):
        pltpu.make_async_remote_copy(
            src_ref=slab.at[lax.rem(virt + step, count_virt)],
            dst_ref=got_line.at[virt],
            send_sem=stage_send.at[3],
            recv_sem=stage_recv.at[3],
            device_id=(pair, lax.rem(virt + step, count_virt)),
            device_id_type=MESH,
        ).start()
    got_line[virt] = slab[virt]
    line = stage(3, count_virt - 1, got_line)
    line.wait_recv()
    for_each(lambda _, rows_in: stage(4, rows_in, got_rows).wait_recv())
    total = jnp.sum(got_rows[...], axis=0) + got_line[0]
    for v in range(1, count_virt):
        total += got_line[v]
    out_ref[...] = total
    for which, target in ((0, got_omega), (1, got_fold), (3, got_two)):
        waiter(which, which * blocks, target, count - 1).wait_send()

    @pl.when(spills)
    def _():
        waiter(2, 2 * blocks, got_spill, owners - 1).wait_send()

    @pl.when(jnp.logical_not(spills))
    def _():
        waiter(2, 2 * blocks, got_spill, owners).wait_send()

    stage(0, count_pair - 1, plane_target).wait_send()
    stage(1, count_virt - 1, line_target).wait_send()
    line.wait_send()

    def sent(strips_out, rows_out):
        stage(2, strips_out, got_plane).wait_send()
        stage(4, rows_out, got_rows).wait_send()

    for_each(sent)


def solution(mesh):
    count_pair, count_virt = mesh.shape["pair"], mesh.shape["virt"]
    count = count_pair * count_virt

    def on_device(amps, two, omega, dipole, occ, orbitals, ospin, vspin):
        width = dipole.shape[0]
        vmem, smem, dma = pltpu.VMEM, pltpu.SMEM, pltpu.SemaphoreType.DMA

        def call(spill, name):
            square = vmem((width, width), HALF)
            got = vmem((count * TILE, LANES), HALF)
            flat = vmem((count, ROWS * 2 * LANES), HALF)
            turned = vmem((ROWS * 2 * LANES, count), HALF)
            return pl.pallas_call(
                functools.partial(kernel, count_pair // 2, count_virt, spill),
                out_shape=(
                    jax.ShapeDtypeStruct((1, count), FULL),
                    jax.ShapeDtypeStruct((1, 1), jnp.int32),
                ),
                in_specs=[pl.BlockSpec(memory_space=pltpu.HBM)] * 8,
                out_specs=(pl.BlockSpec(memory_space=vmem), pl.BlockSpec(memory_space=smem)),
                scratch_shapes=[square] * 10
                + [vmem((spill * TILE, width), HALF)]
                + [got] * 4
                + [flat] * 4
                + [turned] * 2
                + [
                    vmem((count, count), FULL),
                    vmem((count, count), FULL),
                    vmem((count_virt, 1, count), FULL),
                    vmem((count_virt, 1, count), FULL),
                    vmem((count * BLOCK // width, 1, count), FULL),
                    vmem((count * BLOCK // width, 1, count), FULL),
                    smem(occ.shape, occ.dtype),
                    smem(orbitals.shape, orbitals.dtype),
                    smem(ospin.shape, ospin.dtype),
                    vmem((width // LANES, LANES), vspin.dtype),
                    vmem((1, LANES), FULL),
                    vmem((count_pair, 1, LANES), FULL),
                    vmem((1, LANES), FULL),
                    vmem((count_virt, 1, LANES), FULL),
                    vmem((count, LANES), FULL),
                    dma((8,)),
                    dma((4,)),
                    dma((4,)),
                    dma((4 * width // BLOCK,)),
                    dma((5,)),
                    dma((5,)),
                ],
                compiler_params=pltpu.CompilerParams(
                    has_side_effects=True, vmem_limit_bytes=60 * 2**20
                ),
                name=name,
            )

        arrays = (
            amps.reshape(width, width),
            two.reshape(width, width),
            omega.reshape(width, width),
            dipole,
            occ,
            orbitals,
            ospin,
            vspin.reshape(width // LANES, LANES),
        )
        gram, over = call(NARROW, "folded_gram")(*arrays)
        return lax.cond(
            over[0, 0] > 0, lambda _: call(width // TILE, "whole_gram")(*arrays)[0], lambda g: g, gram
        )

    rows = P(("pair", "virt"))
    return jax.shard_map(
        on_device,
        mesh=mesh,
        in_specs=(rows, rows, rows, P(), P(), rows, P(), P()),
        out_specs=P(("pair", "virt"), None),
        check_vma=False,
    )
```

```python
import functools

import jax
import jax.numpy as jnp
from jax import lax
from jax.experimental import pallas as pl
from jax.experimental.pallas import tpu as pltpu
from jax.sharding import PartitionSpec as P

MESH = pl.DeviceIdType.MESH
HALF, FULL = jnp.bfloat16, jnp.float32
ROWS, LANES = 16, 128
TILE = 2 * ROWS
BLOCK = 128
GROUP = 16
NARROW = 4
LAST = (((1,), (1,)), ((), ()))


def kernel(
    rings,
    count_virt,
    spill,
    amps_hbm,
    two_hbm,
    omega_hbm,
    dipole_hbm,
    occ_hbm,
    orb_hbm,
    ospin_hbm,
    vspin_hbm,
    out_ref,
    flag_ref,
    amps,
    dipole,
    omega,
    two,
    place,
    commuted,
    masked,
    put_omega,
    put_two,
    put_fold,
    put_spill,
    got_omega,
    got_two,
    got_fold,
    got_spill,
    left_omega,
    left_two,
    right_masked,
    right_commuted,
    turned_masked,
    turned_commuted,
    partial_sum,
    got_plane,
    slab,
    got_line,
    put_rows,
    got_rows,
    occ,
    orb,
    ospin,
    vspin,
    own_target,
    plane_target,
    row_target,
    line_target,
    targets,
    load_sem,
    own_sem,
    send_sem,
    recv_sem,
    stage_send,
    stage_recv,
):
    pair = lax.axis_index("pair")
    virt = lax.axis_index("virt")
    count_pair = 2 * rings
    count = count_pair * count_virt
    me = pair * count_virt + virt
    width = amps.shape[0]
    strips = width // TILE
    blocks = width // BLOCK
    per_block = strips // blocks
    middle = width // 2

    loads = [
        pltpu.make_async_copy(source, into, load_sem.at[k])
        for k, (source, into) in enumerate(
            (
                (vspin_hbm, vspin),
                (omega_hbm, omega),
                (amps_hbm, amps),
                (dipole_hbm, dipole),
                (two_hbm, two),
                (occ_hbm, occ),
                (orb_hbm, orb),
                (ospin_hbm, ospin),
            )
        )
    ]
    for load in loads:
        load.start()

    def strip_of(p, v):
        ring, core = lax.div(p, 2), lax.rem(p, 2)
        turned = lax.rem(v + ring, count_virt)
        spot = lax.rem(turned, 4) * 4 + core * 2 + lax.div(turned, 4)
        return spot * 2 + lax.div(ring, 8), lax.rem(ring, 8)

    def owner_of(strip, column):
        spot, ring = lax.div(strip, 2), lax.rem(strip, 2) * 8 + column
        turned = lax.rem(spot, 2) * 4 + lax.div(spot, 4)
        return (
            ring * 2 + lax.rem(lax.div(spot, 2), 2),
            lax.rem(turned + count_virt * 2 - ring, count_virt),
        )

    my_strip, my_column = strip_of(pair, virt)
    my_piece = lax.div(pair, count_pair // blocks)
    my_block = lax.div(my_strip, per_block)
    in_piece = count // blocks
    spills = my_strip >= strips - spill

    def tile(ref, strip, column):
        row = pl.multiple_of(strip * TILE, TILE)
        col = pl.multiple_of(column * LANES, LANES)
        return ref.at[pl.ds(row, TILE), pl.ds(col, LANES)]

    def slot(ref, owner):
        return ref.at[pl.ds(pl.multiple_of(owner * TILE, TILE), TILE)]

    def push(which, source, target, strip, column, base, sem):
        p, v = owner_of(strip, column)
        mine = p * count_virt + v == me

        @pl.when(mine)
        def _():
            pltpu.make_async_copy(
                tile(source, strip - base, column), slot(target, me), own_sem.at[which]
            ).start()

        @pl.when(jnp.logical_not(mine))
        def _():
            pltpu.make_async_remote_copy(
                src_ref=tile(source, strip - base, column),
                dst_ref=slot(target, me),
                send_sem=send_sem.at[which],
                recv_sem=recv_sem.at[sem],
                device_id=(p, v),
                device_id_type=MESH,
            ).start()

    turn = lax.div(pair, 2) * 2 + virt * 4

    def send(which, make, source, target, work):
        @pl.loop(0, blocks)
        def _(k):
            block = lax.rem(k + my_piece, blocks)
            make(block)

            @pl.loop(0, per_block * 8)
            def _(i):
                j = lax.rem(i + turn, per_block * 8)
                push(
                    which,
                    source,
                    target,
                    block * per_block + lax.rem(j, 4),
                    lax.div(j, 4),
                    0,
                    which * blocks + my_piece,
                )

            work(k)

    def waiter(which, sem, target, copies):
        part = target.at[pl.ds(0, copies * TILE)]
        return pltpu.make_async_remote_copy(
            src_ref=part,
            dst_ref=part,
            send_sem=send_sem.at[which],
            recv_sem=recv_sem.at[sem],
            device_id=(pair, virt),
            device_id_type=MESH,
        )

    def own_arrived(which, source, target, base):
        pltpu.make_async_copy(
            tile(source, my_strip - base, my_column), slot(target, me), own_sem.at[which]
        ).wait()

    def piece_of(k):
        return lax.rem(my_block + blocks - k, blocks)

    def piece_arrived(which, source, target, piece):
        @pl.when(piece == my_piece)
        def _():
            own_arrived(which, source, target, 0)
            waiter(which, which * blocks + piece, target, in_piece - 1).wait_recv()

        @pl.when(piece != my_piece)
        def _():
            waiter(which, which * blocks + piece, target, in_piece).wait_recv()

    got_plane[...] = jnp.zeros_like(got_plane)
    loads[0].wait()
    spins = vspin[...].astype(FULL)
    before = (
        lax.broadcasted_iota(jnp.int32, (BLOCK, BLOCK), 0)
        < lax.broadcasted_iota(jnp.int32, (BLOCK, BLOCK), 1)
    ).astype(FULL)
    ones_before = jnp.dot(spins, before, preferred_element_type=FULL)
    ones = jnp.zeros((1, 1), FULL)
    lane = lax.broadcasted_iota(jnp.int32, (1, BLOCK), 1)
    goals = []
    for k in range(blocks):
        spin = spins[k : k + 1, :]
        up = (ones_before[k : k + 1, :] + ones).astype(jnp.int32)
        spin_up = spin.astype(jnp.int32)
        rank = jnp.where(spin_up == 1, up, lane + k * BLOCK - up)
        inside = rank < middle
        row = jnp.where(inside, rank, width - 1 - rank)
        bottom = jnp.where(inside, spin_up, 1 - spin_up)
        goals.append(row + (row & -ROWS) + bottom * ROWS)
        ones += jnp.sum(spin, axis=1, keepdims=True)
    zeros = width - ones
    reach = middle + spill * ROWS
    most = jnp.max(jnp.maximum(ones, zeros))
    flag_ref[0, 0] = (most > reach).astype(jnp.int32)

    def make_place(block):
        at = pl.ds(pl.multiple_of(block * BLOCK, BLOCK), BLOCK)
        new_row = lax.broadcasted_iota(jnp.int32, (BLOCK, BLOCK), 0) + block * BLOCK
        for k in range(blocks):
            place[at, k * BLOCK : (k + 1) * BLOCK] = jnp.where(
                new_row == goals[k], 1.0, 0.0
            ).astype(HALF)

    def permuted(block, source):
        at = pl.ds(pl.multiple_of(block * BLOCK, BLOCK), BLOCK)
        return jnp.dot(place[at, :], source[...], preferred_element_type=FULL), at

    def make_from(source, put):
        def make(block):
            moved, at = permuted(block, source)
            put[at, :] = moved.astype(HALF)

        return make

    make_omega = make_from(omega, put_omega)

    def place_and_make(block):
        make_place(block)
        make_omega(block)

    loads[1].wait()
    send(0, place_and_make, put_omega, got_omega, lambda k: None)

    for load in loads[2:]:
        load.wait()
    first, second = orb[0, 0], orb[0, 1]
    shift = occ[first] + occ[second]
    target_spin = (ospin[first] + ospin[second]).astype(FULL)
    def stage(which, copies, ref):
        part = ref.at[pl.ds(0, copies)]
        return pltpu.make_async_remote_copy(
            src_ref=part,
            dst_ref=part,
            send_sem=stage_send.at[which],
            recv_sem=stage_recv.at[which],
            device_id=(pair, virt),
            device_id_type=MESH,
        )

    own_target[...] = jnp.full((1, LANES), 1.0, FULL) * target_spin
    plane_target[pair] = own_target[...]

    @pl.loop(1, count_pair)
    def _(step):
        pltpu.make_async_remote_copy(
            src_ref=own_target,
            dst_ref=plane_target.at[pair],
            send_sem=stage_send.at[0],
            recv_sem=stage_recv.at[0],
            device_id=(lax.rem(pair + step, count_pair), virt),
            device_id_type=MESH,
        ).start()

    all_spins = jnp.concatenate([spins[k : k + 1, :] for k in range(blocks)], axis=1)

    @pl.loop(0, blocks)
    def _(block):
        at = pl.ds(pl.multiple_of(block * BLOCK, BLOCK), BLOCK)
        own = vspin[pl.ds(block, 1), :].astype(FULL)
        column = jnp.broadcast_to(own, (BLOCK, BLOCK)).T[:, 0:1]
        allowed = (column + all_spins) == target_spin
        rows = amps[at, :]
        value = jnp.dot(dipole[at, :], amps[...], preferred_element_type=FULL)
        value += lax.dot_general(rows, dipole[...], LAST, preferred_element_type=FULL)
        wide = rows.astype(FULL)
        value -= shift * wide
        commuted[at, :] = jnp.where(allowed, value, 0.0).astype(HALF)
        masked[at, :] = jnp.where(allowed, wide, 0.0).astype(HALF)

    def make_fold(block):
        row = (
            (block * per_block + lax.broadcasted_iota(jnp.int32, (per_block, ROWS, 1), 0)) * ROWS
            + lax.broadcasted_iota(jnp.int32, (per_block, ROWS, 1), 1)
        ).astype(FULL)
        top_in = row < zeros[:, :, None]
        bottom_in = row < ones[:, :, None]
        kept, over = [], []
        for source in (commuted, masked):
            moved, at = permuted(block, source)
            moved = moved.reshape(per_block, 2, ROWS, width)
            top, bottom = moved[:, 0], moved[:, 1]
            kept.append(jnp.where(top_in, top, 0.0) + jnp.where(bottom_in, bottom, 0.0))
            over.append(jnp.where(top_in, 0.0, top) + jnp.where(bottom_in, 0.0, bottom))
        put_fold[at, :] = jnp.stack(kept, axis=1).reshape(BLOCK, width).astype(HALF)
        first_spill = (strips - spill) // per_block

        @pl.when(block >= first_spill)
        def _():
            to = pl.ds(pl.multiple_of((block - first_spill) * BLOCK, BLOCK), BLOCK)
            put_spill[to, :] = jnp.stack(over, axis=1).reshape(BLOCK, width).astype(HALF)

    @pl.loop(0, blocks)
    def _(block):
        make_fold(block)

    stage(0, count_pair - 1, plane_target).wait_recv()
    gathered = jnp.zeros((1, LANES), FULL)
    for p in range(count_pair):
        gathered = jnp.where(lane == p, plane_target[p], gathered)
    row_target[...] = gathered
    line_target[virt] = gathered
    for step in range(1, count_virt):
        pltpu.make_async_remote_copy(
            src_ref=row_target,
            dst_ref=line_target.at[virt],
            send_sem=stage_send.at[1],
            recv_sem=stage_recv.at[1],
            device_id=(pair, lax.rem(virt + step, count_virt)),
            device_id_type=MESH,
        ).start()
    owners = spill * 8

    @pl.loop(0, owners)
    def _(i):
        j = lax.rem(i + me, owners)
        push(
            2,
            put_spill,
            got_spill,
            strips - spill + lax.div(j, 8),
            lax.rem(j, 8),
            strips - spill,
            2 * blocks,
        )

    size = GROUP * ROWS
    row_id = lax.broadcasted_iota(jnp.int32, (size, size), 0)
    col_id = lax.broadcasted_iota(jnp.int32, (size, size), 1)
    swap = (col_id == (row_id % GROUP) * ROWS + row_id // GROUP).astype(HALF)

    def regrouped(got, g):
        block = got[pl.ds(pl.multiple_of(g * GROUP * TILE, GROUP * TILE), GROUP * TILE), :]
        block = block.reshape(GROUP, 2, ROWS, LANES)
        wide = jnp.concatenate(
            [block[:, 0].reshape(size, LANES), block[:, 1].reshape(size, LANES)], axis=1
        )
        moved = jnp.dot(swap, wide, preferred_element_type=FULL)
        return moved.reshape(ROWS, GROUP, 2 * LANES)

    def regroup(got, into, k):
        for half in range(in_piece // GROUP):
            at = pl.ds(pl.multiple_of(k * in_piece + half * GROUP, GROUP), GROUP)
            moved = regrouped(got, piece_of(k) * (in_piece // GROUP) + half).astype(HALF)
            for r in range(ROWS):
                into[at, r * 2 * LANES : (r + 1) * 2 * LANES] = moved[r]

    def take_omega(k):
        piece_arrived(0, put_omega, got_omega, piece_of(k))
        regroup(got_omega, left_omega, k)

    send(1, lambda block: None, put_fold, got_fold, take_omega)

    stage(1, count_virt - 1, line_target).wait_recv()
    for v in range(count_virt):
        column = jnp.broadcast_to(line_target[v], (LANES, LANES)).T
        targets[pl.ds(v, count_pair, stride=count_virt), :] = column[0:count_pair]
    my_spins = vspin[pl.ds(my_column, 1), :].astype(FULL)

    @pl.when(spills)
    def _():
        own_arrived(2, put_spill, got_spill, strips - spill)
        waiter(2, 2 * blocks, got_spill, count - 1).wait_recv()

    def unfold(g, with_spill):
        at = pl.ds(pl.multiple_of(g * GROUP, GROUP), GROUP)
        target = targets[at, :]
        top = (target == my_spins)[None]
        bottom = (target == my_spins + 1.0)[None]
        main = regrouped(got_fold, g)
        over = regrouped(got_spill, g) if with_spill else None
        for c, into in enumerate((right_commuted, right_masked)):
            half = main[:, :, c * LANES : (c + 1) * LANES]
            rest = over[:, :, c * LANES : (c + 1) * LANES] if with_spill else 0.0
            upper = jnp.where(top, half, jnp.where(bottom, rest, 0.0)).astype(HALF)
            lower = jnp.where(bottom, half, jnp.where(top, rest, 0.0)).astype(HALF)
            for r in range(ROWS):
                into[at, 2 * r * LANES : (2 * r + 1) * LANES] = upper[r]
                into[at, (2 * r + 1) * LANES : (2 * r + 2) * LANES] = lower[r]

    def take_fold(k):
        piece = piece_of(k)
        piece_arrived(1, put_fold, got_fold, piece)
        first_group = piece * (in_piece // GROUP)

        @pl.when(spills)
        def _():
            for half in range(in_piece // GROUP):
                unfold(first_group + half, True)

        @pl.when(jnp.logical_not(spills))
        def _():
            for half in range(in_piece // GROUP):
                unfold(first_group + half, False)

    send(3, make_from(two, put_two), put_two, got_two, take_fold)

    @pl.loop(0, ROWS)
    def _(r):
        at = pl.ds(pl.multiple_of(r * 2 * LANES, 2 * LANES), 2 * LANES)
        for flat, turned in ((right_commuted, turned_commuted), (right_masked, turned_masked)):
            turned[at, :] = flat[:, at].T

    partial_sum[...] = jnp.dot(left_omega[...], turned_masked[...], preferred_element_type=FULL)

    pairs_in_piece = count_pair // blocks

    def rows_of(ref, owner):
        return ref.at[pl.ds(pl.multiple_of(owner * count_virt, count_virt), count_virt)]

    def give(k, u):
        to_pair = piece_of(k) * pairs_in_piece + u
        source = rows_of(partial_sum, k * pairs_in_piece + u)

        @pl.when(to_pair == pair)
        def _():
            rows_of(got_plane, pair)[...] = source[...]

        @pl.when(to_pair != pair)
        def _():
            pltpu.make_async_remote_copy(
                src_ref=source,
                dst_ref=rows_of(got_plane, pair),
                send_sem=stage_send.at[2],
                recv_sem=stage_recv.at[2],
                device_id=(to_pair, virt),
                device_id_type=MESH,
            ).start()

    last = blocks - 1
    for start, stop in ((0, blocks // 2), (blocks // 2, last), (last, blocks)):

        @pl.loop(start, stop)
        def _(k):
            piece_arrived(3, put_two, got_two, piece_of(k))
            regroup(got_two, left_two, k)

        at = slice(start * in_piece, stop * in_piece)
        partial_sum[at, :] = (
            partial_sum[at, :]
            + jnp.dot(left_two[at, :], turned_commuted[...], preferred_element_type=FULL)
        ) * (1.0 / width)
        if start < last:
            for k in range(start, stop):
                for u in range(pairs_in_piece):
                    give(k, u)
        else:
            for i in range(in_piece):
                put_rows[i] = partial_sum[start * in_piece + i : start * in_piece + i + 1, :]

    my_row = lax.rem(my_strip, per_block) * 8 + my_column
    first_pair = piece_of(last) * pairs_in_piece

    @pl.loop(0, in_piece, unroll=4)
    def _(step):
        i = lax.rem(step + my_row, in_piece)
        to_pair, to_virt = first_pair + lax.div(i, count_virt), lax.rem(i, count_virt)
        mine = to_pair * count_virt + to_virt == me

        @pl.when(mine)
        def _():
            got_rows[my_row] = put_rows[i]

        @pl.when(jnp.logical_not(mine))
        def _():
            pltpu.make_async_remote_copy(
                src_ref=put_rows.at[i],
                dst_ref=got_rows.at[my_row],
                send_sem=stage_send.at[4],
                recv_sem=stage_recv.at[4],
                device_id=(to_pair, to_virt),
                device_id_type=MESH,
            ).start()

    straight = piece_of(last) == my_piece
    strips_sent = (count_pair - pairs_in_piece) * count_virt

    def for_each(work):
        @pl.when(straight)
        def _():
            work(strips_sent, in_piece - 1)

        @pl.when(jnp.logical_not(straight))
        def _():
            work(strips_sent - count_virt, in_piece)

    for_each(lambda strips_in, _: stage(2, strips_in, got_plane).wait_recv())
    summed = jnp.sum(got_plane[...].reshape(count_pair, count_virt, count), axis=0)
    for v in range(count_virt):
        slab[v] = summed[v : v + 1, :]

    for step in range(1, count_virt):
        pltpu.make_async_remote_copy(
            src_ref=slab.at[lax.rem(virt + step, count_virt)],
            dst_ref=got_line.at[virt],
            send_sem=stage_send.at[3],
            recv_sem=stage_recv.at[3],
            device_id=(pair, lax.rem(virt + step, count_virt)),
            device_id_type=MESH,
        ).start()
    got_line[virt] = slab[virt]
    line = stage(3, count_virt - 1, got_line)
    line.wait_recv()
    for_each(lambda _, rows_in: stage(4, rows_in, got_rows).wait_recv())
    total = jnp.sum(got_rows[...], axis=0) + got_line[0]
    for v in range(1, count_virt):
        total += got_line[v]
    out_ref[...] = total
    for which, target in ((0, got_omega), (1, got_fold), (3, got_two)):
        waiter(which, which * blocks, target, count - 1).wait_send()

    @pl.when(spills)
    def _():
        waiter(2, 2 * blocks, got_spill, owners - 1).wait_send()

    @pl.when(jnp.logical_not(spills))
    def _():
        waiter(2, 2 * blocks, got_spill, owners).wait_send()

    stage(0, count_pair - 1, plane_target).wait_send()
    stage(1, count_virt - 1, line_target).wait_send()
    line.wait_send()

    def sent(strips_out, rows_out):
        stage(2, strips_out, got_plane).wait_send()
        stage(4, rows_out, got_rows).wait_send()

    for_each(sent)


def solution(mesh):
    count_pair, count_virt = mesh.shape["pair"], mesh.shape["virt"]
    count = count_pair * count_virt

    def on_device(amps, two, omega, dipole, occ, orbitals, ospin, vspin):
        width = dipole.shape[0]
        vmem, smem, dma = pltpu.VMEM, pltpu.SMEM, pltpu.SemaphoreType.DMA

        def call(spill, name):
            square = vmem((width, width), HALF)
            got = vmem((count * TILE, LANES), HALF)
            flat = vmem((count, ROWS * 2 * LANES), HALF)
            turned = vmem((ROWS * 2 * LANES, count), HALF)
            return pl.pallas_call(
                functools.partial(kernel, count_pair // 2, count_virt, spill),
                out_shape=(
                    jax.ShapeDtypeStruct((1, count), FULL),
                    jax.ShapeDtypeStruct((1, 1), jnp.int32),
                ),
                in_specs=[pl.BlockSpec(memory_space=pltpu.HBM)] * 8,
                out_specs=(pl.BlockSpec(memory_space=vmem), pl.BlockSpec(memory_space=smem)),
                scratch_shapes=[square] * 10
                + [vmem((spill * TILE, width), HALF)]
                + [got] * 4
                + [flat] * 4
                + [turned] * 2
                + [
                    vmem((count, count), FULL),
                    vmem((count, count), FULL),
                    vmem((count_virt, 1, count), FULL),
                    vmem((count_virt, 1, count), FULL),
                    vmem((count * BLOCK // width, 1, count), FULL),
                    vmem((count * BLOCK // width, 1, count), FULL),
                    smem(occ.shape, occ.dtype),
                    smem(orbitals.shape, orbitals.dtype),
                    smem(ospin.shape, ospin.dtype),
                    vmem((width // LANES, LANES), vspin.dtype),
                    vmem((1, LANES), FULL),
                    vmem((count_pair, 1, LANES), FULL),
                    vmem((1, LANES), FULL),
                    vmem((count_virt, 1, LANES), FULL),
                    vmem((count, LANES), FULL),
                    dma((8,)),
                    dma((4,)),
                    dma((4,)),
                    dma((4 * width // BLOCK,)),
                    dma((5,)),
                    dma((5,)),
                ],
                compiler_params=pltpu.CompilerParams(
                    has_side_effects=True, vmem_limit_bytes=60 * 2**20
                ),
                name=name,
            )

        arrays = (
            amps.reshape(width, width),
            two.reshape(width, width),
            omega.reshape(width, width),
            dipole,
            occ,
            orbitals,
            ospin,
            vspin.reshape(width // LANES, LANES),
        )
        gram, over = call(NARROW, "folded_gram")(*arrays)
        return lax.cond(
            over[0, 0] > 0, lambda _: call(width // TILE, "whole_gram")(*arrays)[0], lambda g: g, gram
        )

    rows = P(("pair", "virt"))
    return jax.shard_map(
        on_device,
        mesh=mesh,
        in_specs=(rows, rows, rows, P(), P(), rows, P(), P()),
        out_specs=P(("pair", "virt"), None),
        check_vma=False,
    )
```
